512 devices in a mesh: img: 8 (over y, x_lo), gz: 32 (over x_hi, z), gy: 2 (over core).
Axes of the slice: x: 4 (x_hi: 2, x_lo: 2; x = x_hi * 2 + x_lo), y: 4, z: 16, core: 2. Of those that a mesh axis runs over, the one named last changes fastest.
Arguments:
- pixels: bfloat16 [2, 48, 393216], P(None, None, ('img', 'gz', 'gy')), may hold values from -6 to 6
- taps: bfloat16 [9, 393216], P(None, ('img', 'gz', 'gy')), may hold values from 0.099609375 to 1
- plane_offset: int32 [393216], P(('img', 'gz', 'gy')), may hold values from 0 to 15
- grid_row: int32 [393216], P(('img', 'gz', 'gy')), may hold values from 0 to 511
- slab_of_block: int32 [24576, 1], P(('img', 'gz', 'gy')), may hold values from 0 to 31; in each aligned block of 48 rows (0 to 47, 48 to 95, ...) at most 3 rows name the same one
Outputs:
- volume: float32 [2, 48, 512, 512], P(None, ('img', 'gy'), 'gz')
The draws below stay inside these ranges and needn't reach their ends.
Inputs may be any that keep to these rules, and one draw needn't show every extreme that they name: `slab_of_block`: within the 48 blocks of one device no slab is named by more than 3 blocks, and on some devices one slab is named by exactly 3 blocks.
All inputs are finite; a program needn't handle non-finite values.
Results may differ from the reference program's by a relative error of at most 0.004.
Values may be sent and summed in bfloat16 or wider, within the bound.
A program may use at most 64 MiB of HBM per device.

```python
import math
import jax
import jax.numpy as jnp
import numpy as np

NB = 48
BR = 16
SZ = 16
NY = 512
XW = 48
CAPB = 3
NZ = 512
BLOCKS = 24576
ROWS = 393216
N_GZ = 32


def set_ends(result, own_key, least, largest):
    index_at = [jax.random.randint(jax.random.fold_in(own_key, axis), (), 0, length) for axis, length in enumerate(result.shape)]
    longest = result.shape.index(max(result.shape))
    beside = index_at[:longest] + [(index_at[longest] + 1) % result.shape[longest]] + index_at[longest + 1:]
    return result.at[tuple(index_at)].set(least).at[tuple(beside)].set(largest)


def block_scale(rng, shape, pieces, least, high):
    def one(dim, blocks):
        steps = jax.random.uniform(jax.random.fold_in(jax.random.fold_in(rng, 6), dim), (blocks,), jnp.float32, least / len(pieces), high / len(pieces))
        return jnp.repeat(jnp.exp(steps), shape[dim] // blocks).reshape((-1,) + (1,) * (len(shape) - dim - 1))

    gain = one(*pieces[0])
    for cut in pieces[1:]:
        gain = gain * one(*cut)
    return gain


def shared_out(own_key, own, number, rows, number_of, top, bound, lean):
    sequence = jax.random.permutation(own_key, number_of)
    heavy_load, ordinary = portions_of(number_of, rows * top, bound, lean, True), portions_of(number_of, rows * top, bound, lean, False)
    places = jnp.arange(number_of)

    def named(tallies, turn):
        used = int((tallies > 0).sum())
        fixed = max(1, used // 4)
        shifted = fixed + (places - fixed + turn * (used - fixed)) % max(1, number_of - fixed)
        return jnp.zeros((number_of,), jnp.int32).at[sequence[jnp.where(places < fixed, places, shifted)]].set(jnp.asarray(tallies, jnp.int32))

    tallies = jnp.where(number % 4 == 0, named(heavy_load, number // 4), named(ordinary, number - number // 4 - 1))
    mixed = jax.random.permutation(jax.random.fold_in(own, 3), number_of)
    giver, receiver = mixed[0:number_of // 2 * 2:2], mixed[1:number_of // 2 * 2:2]
    slack = jnp.minimum(tallies[giver] - 1, bound - tallies[receiver]) // 2
    slack = jnp.where((giver == sequence[0]) | (receiver == sequence[0]) | (tallies[receiver] == 0), 0, jnp.maximum(slack, 0))
    shifted = jax.random.randint(jax.random.fold_in(own, 4), (number_of // 2,), 0, 1 << 20) % (slack + 1)
    tallies = tallies.at[giver].add(-shifted).at[receiver].add(shifted)
    members = jnp.searchsorted(jnp.cumsum(tallies), jnp.arange(rows * top), side="right").astype(jnp.int32)
    table = members.reshape(top, rows).T
    table = table[jax.random.permutation(jax.random.fold_in(own, 1), rows)]
    turn = jax.random.randint(jax.random.fold_in(own, 2), (rows, 1), 0, top)
    return jnp.take_along_axis(table, (jnp.arange(top)[None, :] + turn) % top, axis=1)


def portions_of(number_of, total, most, skew, full):
    loads = [(1 << 20) // math.isqrt(rank ** skew) + 1 for rank in range(1, number_of + 1)]
    largest = most if full else min(most, max(-(-total // number_of), total * loads[0] // sum(loads)))
    least = 1 if total - largest >= number_of - 1 else 0
    holding, rest = [largest] + [least] * (number_of - 1), total - largest - least * (number_of - 1)
    while rest > 0:
        movable = [i for i in range(1, number_of) if holding[i] < largest] or [i for i in range(1, number_of) if holding[i] < most]
        mass, remaining = sum([loads[i] for i in movable]), rest
        for i in movable:
            more = min(most - holding[i], max(1, remaining * loads[i] // mass), rest)
            holding[i] = holding[i] + more
            rest = rest - more
    return np.array(holding)


def noise(stream_key, shape, width, most, pieces=(), kind=jnp.bfloat16):
    drawn = width * jax.random.normal(stream_key, shape, jnp.float32)
    if pieces:
        drawn = drawn * block_scale(stream_key, shape, pieces, -0.22, 0.18)
    return jnp.clip(drawn, -most, most).astype(kind)


def setup_inputs(seed: int = 0) -> dict:
    key_of = jax.random.split(jax.random.key(seed), 6)
    pixels = noise(key_of[0], (2, XW, ROWS), 1.0, 6.0, ((2, 512),))
    taps = jnp.clip(0.099609375 + 0.9003906 * jax.random.uniform(key_of[1], (9, ROWS), jnp.float32) ** block_scale(key_of[1], (9, ROWS), ((1, 512),), -0.2, 0.2), 0.099609375, 1.0).astype(jnp.bfloat16)
    plane_offset = set_ends(jax.random.randint(key_of[2], (ROWS,), 0, SZ), jax.random.fold_in(key_of[2], 1), 0, SZ - 1).astype(jnp.int32)
    grid_row = set_ends(jax.random.randint(key_of[3], (ROWS,), 0, NY), jax.random.fold_in(key_of[3], 1), 0, NY - 1).astype(jnp.int32)
    slab_of_block_keys = jax.random.split(jax.random.fold_in(key_of[4], 1), BLOCKS // NB)
    slab_of_block_turns = jax.random.permutation(jax.random.fold_in(key_of[4], 3), BLOCKS // NB)
    slab_of_block = jax.vmap(lambda own, number: shared_out(jax.random.fold_in(key_of[4], 2), own, number, NB, N_GZ, 1, CAPB, 2))(slab_of_block_keys, slab_of_block_turns).reshape((BLOCKS, 1))
    return dict(pixels=pixels, taps=taps, plane_offset=plane_offset, grid_row=grid_row, slab_of_block=slab_of_block)


def reference(pixels, taps, plane_offset, grid_row, slab_of_block):
    tap_values = taps.astype(jnp.float32)
    padded = jnp.pad(pixels.astype(jnp.float32), ((0, 0), (1, 1), (0, 0)))
    spread = tap_values[6] * padded[:, :-2] + tap_values[7] * padded[:, 1:-1] + tap_values[8] * padded[:, 2:]
    spread = spread.astype(jnp.bfloat16).astype(jnp.float32)
    values = jnp.transpose(spread, (2, 0, 1))
    slab_rows = jnp.repeat(slab_of_block[:, 0], BR)
    base_plane = slab_rows * SZ + plane_offset
    grid = jnp.zeros((NZ, NY, 2, XW), jnp.float32)
    for a in range(3):
        for b in range(3):
            weight = (tap_values[a] * tap_values[3 + b]).astype(jnp.bfloat16).astype(jnp.float32)
            plane_index = ((base_plane + a) % NZ).astype(jnp.int32)
            row_index = ((grid_row + b - 1) % NY).astype(jnp.int32)
            grid = grid.at[plane_index, row_index].add(weight[:, None, None] * values)
    field = grid[:, :, 0] + 1j * grid[:, :, 1]
    volume = jnp.fft.ifft2(field, axes=(0, 1), norm="ortho")
    parts = jnp.stack([jnp.real(volume), jnp.imag(volume)]).astype(jnp.float32)
    return jnp.transpose(parts, (0, 3, 2, 1))
```

```python
import functools
import math

import jax
import jax.numpy as jnp
import numpy as np
from jax import lax
from jax.experimental import pallas as pl
from jax.experimental.pallas import tpu as pltpu
from jax.sharding import PartitionSpec as P

MESH = pl.DeviceIdType.MESH
F32 = jnp.float32
BF16 = jnp.bfloat16
TILE = 16
CAPACITY = 3
META = 8
LANES = 128
NT = (((1,), (1,)), ((), ()))


def transform_table(length):
    steps = np.arange(length)
    phase = (steps[:, None] * steps[None, :] % length) * (2.0 * math.pi / length)
    table = np.concatenate([np.cos(phase), np.sin(phase)], axis=1) / math.sqrt(length)
    table = table.astype(np.float32)
    high = table.astype(jnp.bfloat16)
    low = (table - high.astype(np.float32)).astype(jnp.bfloat16)
    return np.stack([high, low])


def pick_table(width, groups):
    columns = width // groups
    pick = np.zeros((groups, TILE, LANES), np.float32)
    for group in range(groups):
        for s in range(2 * columns):
            pick[group, s, (s % 2) * width + group * columns + s // 2] = 1.0
        for s in range(META):
            pick[group, 2 * columns + s, 2 * width + s] = 1.0
    return pick.reshape(groups * TILE, LANES).astype(jnp.bfloat16)


def rim_table(columns):
    place = np.zeros((LANES, LANES), np.float32)
    for x in range(columns):
        for c in range(2):
            for z in range(2):
                place[2 * columns * TILE + TILE * c + 2 * x + z, (2 * x + c) * TILE + z] = 1.0
    return place.astype(jnp.bfloat16)


def kernel(
    sizes, pix_ref, taps_ref, plane_ref, row_ref, slab_ref, pick_ref, rim_ref, table_hbm, out_ref,
    x_buf, send1, recv1, send2, recv2, acc, table, send3, recv3,
    s1_sem, r1_sem, s2_sem, r2_sem, s3_sem, r3_sem, table_sem,
):
    n_img, n_gz, n_gy, width, ny, parts, step = sizes
    nx_hi = 2
    nz = n_gz // nx_hi
    groups = n_img * n_gy
    columns = width // groups
    rows = pix_ref.shape[2]
    blocks = rows // TILE
    slot_rows = CAPACITY * TILE
    part_slots = n_gz // parts
    part_rows = part_slots * slot_rows
    half = ny // 2

    img, gz, gy = lax.axis_index("img"), lax.axis_index("gz"), lax.axis_index("gy")
    my_group = img * n_gy + gy

    def slab_peer(k):
        turn, m = k % nx_hi, k // nx_hi
        along = ((m + 1) // 2) * (2 * (m % 2) - 1)
        z = (gz % nz + along + nz) % nz
        x = (gz // nz + turn) % nx_hi
        return x * nz + z

    def group_peer(e):
        core, rest = e % n_gy, e // n_gy
        side, along = rest % 2, rest // 2
        y = (img // 2 + along) % (n_img // 2)
        x = (img % 2 + side) % 2
        return y * 2 + x, (gy + core) % n_gy

    def copy1(k):
        peer = slab_peer(k)
        return pltpu.make_async_remote_copy(
            src_ref=send1.at[pl.ds(pl.multiple_of(peer * slot_rows, TILE), slot_rows)],
            dst_ref=recv1.at[pl.ds(pl.multiple_of(k * slot_rows, TILE), slot_rows)],
            send_sem=s1_sem.at[k], recv_sem=r1_sem.at[k],
            device_id=(img, peer, gy), device_id_type=MESH,
        )

    def copy2(part, e):
        to_img, to_gy = group_peer(e)
        peer = to_img * n_gy + to_gy
        return pltpu.make_async_remote_copy(
            src_ref=send2.at[part, pl.ds(pl.multiple_of(peer * TILE, TILE), TILE)],
            dst_ref=recv2.at[part, e],
            send_sem=s2_sem.at[part, e], recv_sem=r2_sem.at[part, e],
            device_id=(to_img, gz, to_gy), device_id_type=MESH,
        )

    def copy3(k):
        peer = slab_peer(k)
        return pltpu.make_async_remote_copy(
            src_ref=send3.at[pl.ds(pl.multiple_of(peer * TILE, TILE), TILE)],
            dst_ref=recv3.at[pl.ds(pl.multiple_of(gz * TILE, TILE), TILE)],
            send_sem=s3_sem.at[k], recv_sem=r3_sem.at[k],
            device_id=(img, peer, gy), device_id_type=MESH,
        )

    def loop(first, last, do):
        def body(index, carry):
            do(index)
            return carry
        lax.fori_loop(first, last, body, 0)

    barrier = pltpu.get_barrier_semaphore()

    def greet_slab(k):
        pl.semaphore_signal(barrier, inc=1, device_id=(img, slab_peer(k), gy), device_id_type=MESH)

    def greet_group(e):
        to_img, to_gy = group_peer(e)
        pl.semaphore_signal(barrier, inc=1, device_id=(to_img, gz, to_gy), device_id_type=MESH)

    loop(1, n_gz, greet_slab)
    loop(1, groups, greet_group)

    table_copy = pltpu.make_async_copy(table_hbm, table, table_sem)
    table_copy.start()

    taps = taps_ref[...].astype(F32)
    x_iota = lax.broadcasted_iota(jnp.int32, (width, rows), 0)
    for c in range(2):
        p = pix_ref[c].astype(F32)
        before = jnp.where(x_iota == 0, 0.0, pltpu.roll(p, 1, 0))
        after = jnp.where(x_iota == width - 1, 0.0, pltpu.roll(p, width - 1, 0))
        spread = taps[6:7] * before + taps[7:8] * p + taps[8:9] * after
        x_buf[c * width : (c + 1) * width] = spread.astype(BF16)
    data = jnp.concatenate(
        [
            taps[0:6], plane_ref[...].astype(F32), (row_ref[...] - half).astype(F32),
            jnp.zeros((LANES - 2 * width - META, rows), F32),
        ],
        axis=0,
    )
    x_buf[2 * width :] = data.astype(BF16)

    block_iota = lax.broadcasted_iota(jnp.int32, (blocks, rows), 0)
    row_iota = lax.broadcasted_iota(jnp.int32, (blocks, rows), 1)
    row_block = row_iota // TILE
    target = jnp.broadcast_to(slab_ref[...], (blocks, rows))
    own = jnp.sum(jnp.where(block_iota == row_block, target, 0), axis=0, keepdims=True)
    earlier = jnp.where((target == own) & (block_iota < row_block), 1, 0)
    rank = jnp.sum(earlier, axis=0, keepdims=True)
    place = (own * CAPACITY + rank) * TILE + row_iota[0:1] % TILE

    slot_iota = lax.broadcasted_iota(jnp.int32, (LANES, rows), 0)

    def permute(index):
        first = pl.multiple_of(index * LANES, LANES)
        chosen = jnp.where(slot_iota == place - first, 1.0, 0.0).astype(BF16)
        moved = lax.dot_general(chosen, x_buf[...], NT, preferred_element_type=F32)
        send1[pl.ds(first, LANES)] = moved.astype(BF16)

    loop(0, n_gz * slot_rows // LANES, permute)

    pl.semaphore_wait(barrier, n_gz + groups - 2)
    loop(1, n_gz, lambda k: copy1(k).start())
    recv1[0:slot_rows] = send1[pl.ds(pl.multiple_of(gz * slot_rows, TILE), slot_rows)]

    acc[...] = jnp.zeros_like(acc)
    y_iota = lax.broadcasted_iota(jnp.int32, (half + TILE, step), 0).astype(F32)
    z_iota = lax.broadcasted_iota(jnp.int32, (TILE, step), 0)
    rim_x = z_iota // 2
    rim_z = (z_iota % 2 + TILE).astype(F32)
    z_iota = z_iota.astype(F32)

    def spread_part(part, index):
        e, first = index // (part_rows // step), index % (part_rows // step)
        got = recv2[part, e, :, pl.ds(pl.multiple_of(first * step, step), step)].astype(F32)
        plane = got[12:13]
        y = got[13:14] + (half - 1.0)
        y = jnp.where(y < 0.0, y + ny, y)
        upper = y >= half
        y = jnp.where(upper, y - half, y)
        along_y = jnp.where(
            y_iota == y, got[9:10],
            jnp.where(y_iota == y + 1.0, got[10:11], jnp.where(y_iota == y + 2.0, got[11:12], 0.0)),
        ).astype(BF16)
        along_z = jnp.where(
            z_iota == plane, got[6:7],
            jnp.where(
                z_iota == plane + 1.0, got[7:8], jnp.where(z_iota == plane + 2.0, got[8:9], 0.0)
            ),
        )
        rim = jnp.where(
            rim_z == plane + 1.0, got[7:8], jnp.where(rim_z == plane + 2.0, got[8:9], 0.0)
        )
        pieces = [along_z * got[s : s + 1] for s in range(2 * columns)]
        for c in range(2):
            value = jnp.zeros((TILE, step), F32)
            for x in range(columns):
                value = jnp.where(rim_x == x, got[2 * x + c : 2 * x + c + 1], value)
            pieces.append(rim * value)
        pieces = [jnp.where(upper, 0.0, piece) for piece in pieces] + [
            jnp.where(upper, piece, 0.0) for piece in pieces
        ]
        along_zx = jnp.concatenate([piece.astype(BF16) for piece in pieces], axis=0)
        acc[...] += lax.dot_general(along_y, along_zx, NT, preferred_element_type=F32)

    def take_part(part):
        def arrived(k):
            copy1(k).wait_recv()
        loop(jnp.maximum(part * part_slots, 1), (part + 1) * part_slots, arrived)
        first = pl.multiple_of(part * part_rows, TILE)
        turned = lax.dot_general(
            pick_ref[...], recv1[pl.ds(first, part_rows)], NT, preferred_element_type=F32
        )
        send2[part] = turned.astype(BF16)
        loop(1, groups, lambda e: copy2(part, e).start())
        recv2[part, 0] = send2[part, pl.ds(pl.multiple_of(my_group * TILE, TILE), TILE)]

    def grid_part(part):
        loop(1, groups, lambda e: copy2(part, e).wait_recv())
        loop(0, groups * part_rows // step, functools.partial(spread_part, part))

    def pipeline(part):
        take_part(part)
        grid_part(part - 1)

    take_part(0)
    loop(1, parts, pipeline)
    grid_part(parts - 1)

    table_copy.wait()
    lane = lax.broadcasted_iota(jnp.int32, (ny, LANES), 1)
    low, high = acc[:half, :LANES], acc[:half, LANES:]
    low_rim, high_rim = acc[half:, :LANES], acc[half:, LANES:]
    grid = jnp.concatenate(
        [low[:TILE] + high_rim, low[TILE:], high[:TILE] + low_rim, high[TILE:]], axis=0
    )
    other = jnp.where(
        (lane // TILE) % 2 == 0, -pltpu.roll(grid, LANES - TILE, 1), pltpu.roll(grid, TILE, 1)
    )
    both = jnp.concatenate([grid, other], axis=0)
    both_high = both.astype(BF16)
    both_low = (both - both_high.astype(F32)).astype(BF16)
    both_bits = jnp.concatenate([both_high, both_low], axis=1)
    wide = jnp.dot(table[0], both_bits, preferred_element_type=F32)
    turned = wide[:, :LANES] + wide[:, LANES:]
    turned = turned + jnp.dot(table[1], both_high, preferred_element_type=F32)
    send3[...] = turned.astype(BF16)

    loop(1, n_gz, lambda k: copy3(k).start())
    here = pl.ds(pl.multiple_of(gz * TILE, TILE), TILE)
    recv3[here] = send3[here]
    loop(1, n_gz, lambda k: copy3(k).wait_recv())

    got = recv3[...]
    past = jnp.dot(got, rim_ref[...], preferred_element_type=F32)
    planes = got.astype(F32) + jnp.concatenate([past[-TILE:], past[:-TILE]], axis=0)
    per = LANES // TILE
    spot = lax.broadcasted_iota(jnp.int32, (TILE, LANES), 1) // TILE
    ordered = []
    for s in range(2 * columns):
        across = []
        for t in range(n_gz // per):
            value = jnp.zeros((TILE, LANES), F32)
            for j in range(per):
                first = (t * per + j) * TILE
                tile = planes[first : first + TILE]
                turn = (j - s) * TILE % LANES
                tile = pltpu.roll(tile, turn, 1) if turn else tile
                value = jnp.where(spot == j, tile, value)
            across.append(value.astype(BF16))
        ordered.append(jnp.concatenate(across, axis=1))
    ordered = jnp.concatenate(ordered, axis=0)
    volume = jnp.dot(ordered, table[0], preferred_element_type=F32)
    volume = volume + jnp.dot(ordered, table[1], preferred_element_type=F32)
    for x in range(columns):
        real = volume[2 * x * TILE : (2 * x + 1) * TILE]
        imag = volume[(2 * x + 1) * TILE : (2 * x + 2) * TILE]
        out_ref[0, x] = real[:, :ny] - imag[:, ny:]
        out_ref[1, x] = real[:, ny:] + imag[:, :ny]

    loop(1, n_gz, lambda k: copy1(k).wait_send())
    loop(0, parts, lambda part: loop(1, groups, lambda e: copy2(part, e).wait_send()))
    loop(1, n_gz, lambda k: copy3(k).wait_send())


def local(sizes, pixels, taps, plane_offset, grid_row, slab_of_block):
    n_img, n_gz, n_gy, width, ny, parts, step = sizes
    groups = n_img * n_gy
    columns = width // groups
    rows = pixels.shape[2]
    slots = n_gz * CAPACITY * TILE
    vmem = pl.BlockSpec(memory_space=pltpu.VMEM)
    return pl.pallas_call(
        functools.partial(kernel, sizes),
        out_shape=jax.ShapeDtypeStruct((2, columns, ny // n_gz, ny), F32),
        in_specs=[vmem] * 7 + [pl.BlockSpec(memory_space=pl.ANY)],
        out_specs=vmem,
        scratch_shapes=[
            pltpu.VMEM((LANES, rows), BF16),
            pltpu.VMEM((slots, LANES), BF16),
            pltpu.VMEM((slots, LANES), BF16),
            pltpu.VMEM((parts, groups * TILE, slots // parts), BF16),
            pltpu.VMEM((parts, groups, TILE, slots // parts), BF16),
            pltpu.VMEM((ny // 2 + TILE, 2 * LANES), F32),
            pltpu.VMEM((2, ny, 2 * ny), BF16),
            pltpu.VMEM((ny, LANES), BF16),
            pltpu.VMEM((ny, LANES), BF16),
            pltpu.SemaphoreType.DMA((n_gz,)),
            pltpu.SemaphoreType.DMA((n_gz,)),
            pltpu.SemaphoreType.DMA((parts, groups)),
            pltpu.SemaphoreType.DMA((parts, groups)),
            pltpu.SemaphoreType.DMA((n_gz,)),
            pltpu.SemaphoreType.DMA((n_gz,)),
            pltpu.SemaphoreType.DMA,
        ],
        compiler_params=pltpu.CompilerParams(
            collective_id=0, has_side_effects=True, vmem_limit_bytes=48 * 1024 * 1024
        ),
    )(
        pixels, taps, plane_offset.reshape(1, rows), grid_row.reshape(1, rows), slab_of_block,
        jnp.asarray(pick_table(width, groups)), jnp.asarray(rim_table(columns)),
        jnp.asarray(transform_table(ny)),
    )


def solution(mesh, width=48, ny=512, parts=4, step=384):
    sizes = (mesh.shape["img"], mesh.shape["gz"], mesh.shape["gy"], width, ny, parts, step)
    return jax.shard_map(
        functools.partial(local, sizes),
        mesh=mesh,
        in_specs=(
            P(None, None, ("img", "gz", "gy")),
            P(None, ("img", "gz", "gy")),
            P(("img", "gz", "gy")),
            P(("img", "gz", "gy")),
            P(("img", "gz", "gy"), None),
        ),
        out_specs=P(None, ("img", "gy"), "gz", None),
        check_vma=False,
    )
```

```python
import functools
import math

import jax
import jax.numpy as jnp
import numpy as np
from jax import lax
from jax.experimental import pallas as pl
from jax.experimental.pallas import tpu as pltpu
from jax.sharding import PartitionSpec as P

MESH = pl.DeviceIdType.MESH
F32 = jnp.float32
BF16 = jnp.bfloat16
TILE = 16
CAPACITY = 3
META = 8
LANES = 128
NT = (((1,), (1,)), ((), ()))


def transform_table(length):
    steps = np.arange(length)
    phase = (steps[:, None] * steps[None, :] % length) * (2.0 * math.pi / length)
    table = np.concatenate([np.cos(phase), np.sin(phase)], axis=1) / math.sqrt(length)
    table = table.astype(np.float32)
    high = table.astype(jnp.bfloat16)
    low = (table - high.astype(np.float32)).astype(jnp.bfloat16)
    return np.stack([high, low])


def pick_table(width, groups):
    columns = width // groups
    pick = np.zeros((groups, TILE, LANES), np.float32)
    for group in range(groups):
        for s in range(2 * columns):
            pick[group, s, (s % 2) * width + group * columns + s // 2] = 1.0
        for s in range(META):
            pick[group, 2 * columns + s, 2 * width + s] = 1.0
    return pick.reshape(groups * TILE, LANES).astype(jnp.bfloat16)


def rim_table(columns):
    place = np.zeros((LANES, LANES), np.float32)
    for x in range(columns):
        for c in range(2):
            for z in range(2):
                place[2 * columns * TILE + TILE * c + 2 * x + z, (2 * x + c) * TILE + z] = 1.0
    return place.astype(jnp.bfloat16)


def kernel(
    sizes, pix_hbm, taps_hbm, plane_hbm, row_hbm, slab_hbm, small_hbm, table_hbm, out_ref,
    pix_ref, taps_ref, plane_ref, row_ref, slab_ref, small, x_buf, send1, recv1, send2, recv2, acc, table, send3, recv3,
    s1_sem, r1_sem, s2_sem, r2_sem, s3_sem, r3_sem, in_sem,
):
    n_img, n_gz, n_gy, width, ny, parts, step = sizes
    nx_hi = 2
    nz = n_gz // nx_hi
    groups = n_img * n_gy
    columns = width // groups
    rows = pix_hbm.shape[2]
    blocks = rows // TILE
    slot_rows = CAPACITY * TILE
    part_slots = n_gz // parts
    part_rows = part_slots * slot_rows
    half = ny // 2
    FAR, FIRST, LAST, OWN = True, 0, n_gz - 1, n_gz - 1

    img, gz, gy = lax.axis_index("img"), lax.axis_index("gz"), lax.axis_index("gy")
    my_group = img * n_gy + gy

    def slab_peer(k):
        k = n_gz - 1 - k if FAR else k
        turn, m = k % nx_hi, k // nx_hi
        along = ((m + 1) // 2) * (2 * (m % 2) - 1)
        z = (gz % nz + along + nz) % nz
        x = (gz // nz + turn) % nx_hi
        return x * nz + z

    def group_peer(e):
        core, rest = e % n_gy, e // n_gy
        side, along = rest % 2, rest // 2
        y = (img // 2 + along) % (n_img // 2)
        x = (img % 2 + side) % 2
        return y * 2 + x, (gy + core) % n_gy

    def copy1(k):
        peer = slab_peer(k)
        return pltpu.make_async_remote_copy(
            src_ref=send1.at[pl.ds(pl.multiple_of(k * slot_rows, TILE), slot_rows)],
            dst_ref=recv1.at[pl.ds(pl.multiple_of(k * slot_rows, TILE), slot_rows)],
            send_sem=s1_sem.at[k], recv_sem=r1_sem.at[k],
            device_id=(img, peer, gy), device_id_type=MESH,
        )

    def copy2(part, e):
        to_img, to_gy = group_peer(e)
        peer = to_img * n_gy + to_gy
        return pltpu.make_async_remote_copy(
            src_ref=send2.at[part, pl.ds(pl.multiple_of(peer * TILE, TILE), TILE)],
            dst_ref=recv2.at[part, :, pl.ds(pl.multiple_of(e * part_rows, LANES), part_rows)],
            send_sem=s2_sem.at[part, e], recv_sem=r2_sem.at[part, e],
            device_id=(to_img, gz, to_gy), device_id_type=MESH,
        )

    def copy3(index):
        peer = index % nx_hi * nz + index // nx_hi
        return pltpu.make_async_remote_copy(
            src_ref=send3.at[pl.ds(pl.multiple_of(peer * TILE, TILE), TILE)],
            dst_ref=recv3.at[pl.ds(pl.multiple_of(gz * TILE, TILE), TILE)],
            send_sem=s3_sem.at[peer], recv_sem=r3_sem.at[gz],
            device_id=(img, peer, gy), device_id_type=MESH,
        )

    def loop(first, last, do):
        def body(index, carry):
            do(index)
            return carry
        lax.fori_loop(first, last, body, 0)

    pairs = [
        (slab_hbm, slab_ref), (taps_hbm, taps_ref), (plane_hbm, plane_ref), (row_hbm, row_ref),
        (pix_hbm, pix_ref), (small_hbm, small), (table_hbm, table),
    ]
    fetches = [pltpu.make_async_copy(*pair, in_sem.at[i]) for i, pair in enumerate(pairs)]
    for fetch in fetches:
        fetch.start()

    def arrival3(peer):
        here = recv3.at[pl.ds(pl.multiple_of(peer * TILE, TILE), TILE)]
        return pltpu.make_async_remote_copy(
            src_ref=here, dst_ref=here, send_sem=s3_sem.at[0], recv_sem=r3_sem.at[peer],
            device_id=(img, peer, gy), device_id_type=MESH,
        )

    def others(first, last, mine, do):
        def step_of(index):
            @pl.when(index != mine)
            def _():
                do(index)
        loop(first, last, step_of)

    barrier = pltpu.get_barrier_semaphore()

    def greet_slab(k):
        pl.semaphore_signal(barrier, inc=1, device_id=(img, slab_peer(k), gy), device_id_type=MESH)

    def greet_group(e):
        to_img, to_gy = group_peer(e)
        pl.semaphore_signal(barrier, inc=1, device_id=(to_img, gz, to_gy), device_id_type=MESH)

    loop(FIRST, LAST, greet_slab)
    loop(1, groups, greet_group)


    for fetch in fetches[:5]:
        fetch.wait()
    taps = taps_ref[...].astype(F32)
    x_iota = lax.broadcasted_iota(jnp.int32, (width, rows), 0)
    for c in range(2):
        p = pix_ref[c].astype(F32)
        before = jnp.where(x_iota == 0, 0.0, pltpu.roll(p, 1, 0))
        after = jnp.where(x_iota == width - 1, 0.0, pltpu.roll(p, width - 1, 0))
        spread = taps[6:7] * before + taps[7:8] * p + taps[8:9] * after
        x_buf[c * width : (c + 1) * width] = spread.astype(BF16)
    data = jnp.concatenate(
        [
            taps[0:6], plane_ref[...].reshape(1, rows).astype(F32),
            (row_ref[...].reshape(1, rows) - half).astype(F32),
            jnp.zeros((LANES - 2 * width - META, rows), F32),
        ],
        axis=0,
    )
    x_buf[2 * width :] = data.astype(BF16)

    block_iota = lax.broadcasted_iota(jnp.int32, (blocks, rows), 0)
    row_iota = lax.broadcasted_iota(jnp.int32, (blocks, rows), 1)
    row_block = row_iota // TILE
    square = (blocks, blocks)
    diagonal = lax.broadcasted_iota(jnp.int32, square, 0) == lax.broadcasted_iota(jnp.int32, square, 1)
    target = jnp.sum(jnp.where(diagonal, slab_ref[...], 0), axis=1, keepdims=True)
    target = jnp.broadcast_to(target, (blocks, rows))
    own = jnp.sum(jnp.where(block_iota == row_block, target, 0), axis=0, keepdims=True)
    earlier = jnp.where((target == own) & (block_iota < row_block), 1, 0)
    rank = jnp.sum(earlier, axis=0, keepdims=True)
    turn = (own // nz - gz // nz + nx_hi) % nx_hi
    along = (own % nz - gz % nz + nz) % nz
    order = jnp.where(along == 0, 0, jnp.where(along <= nz // 2, 2 * along - 1, 2 * (nz - along)))
    order = order * nx_hi + turn
    order = n_gz - 1 - order if FAR else order
    place = (order * CAPACITY + rank) * TILE + row_iota[0:1] % TILE

    slot_iota = lax.broadcasted_iota(jnp.int32, (part_rows, rows), 0)
    pl.semaphore_wait(barrier, n_gz + groups - 2)

    def permute(index):
        first = pl.multiple_of(index * part_rows, LANES)
        chosen = jnp.where(slot_iota == place - first, 1.0, 0.0).astype(BF16)
        moved = lax.dot_general(chosen, x_buf[...], NT, preferred_element_type=F32)
        send1[pl.ds(first, part_rows)] = moved.astype(BF16)
        loop(
            jnp.maximum(index * part_slots, FIRST), jnp.minimum((index + 1) * part_slots, LAST),
            lambda k: copy1(k).start(),
        )

    loop(0, parts, permute)
    own_slot = OWN * slot_rows
    recv1[own_slot : own_slot + slot_rows] = send1[own_slot : own_slot + slot_rows]

    acc[...] = jnp.zeros_like(acc)
    y_iota = (lax.broadcasted_iota(jnp.int32, (half + TILE, step), 0) - half // 2).astype(BF16)
    z_iota = lax.broadcasted_iota(jnp.int32, (TILE, step), 0)
    rim_x = z_iota // 2
    rim_z = (z_iota % 2 + TILE).astype(BF16)
    z_iota = z_iota.astype(BF16)

    def spread_part(part, index):
        got = recv2[part, :, pl.ds(pl.multiple_of(index * step, step), step)]
        zero = jnp.zeros((), BF16)
        y = got[13:14].astype(F32) + (half - 1.0)
        y = jnp.where(y < 0.0, y + ny, y)
        upper = y >= half
        y = jnp.where(upper, y - half, y) - half // 2
        ys = [(y + b).astype(BF16) for b in range(3)]
        in_high = jnp.where(upper, 1.0, 0.0).astype(BF16)
        got = got.astype(BF16)
        z0 = got[12:13]
        z1, z2 = z0 + 1, z0 + 2
        along_y = jnp.where(
            y_iota == ys[0], got[9:10],
            jnp.where(y_iota == ys[1], got[10:11], jnp.where(y_iota == ys[2], got[11:12], zero)),
        ).astype(BF16)
        along_z = jnp.where(
            z_iota == z0, got[6:7],
            jnp.where(z_iota == z1, got[7:8], jnp.where(z_iota == z2, got[8:9], zero)),
        )
        rim = jnp.where(rim_z == z1, got[7:8], jnp.where(rim_z == z2, got[8:9], zero))
        values = []
        for c in range(2):
            value = jnp.zeros((TILE, step), BF16)
            for x in range(columns):
                value = jnp.where(rim_x == x, got[2 * x + c : 2 * x + c + 1], value)
            values.append(value)
        pieces = []
        for mask in (1 - in_high, in_high):
            z_part, rim_part = along_z * mask, rim * mask
            pieces += [z_part * got[s : s + 1] for s in range(2 * columns)]
            pieces += [rim_part * value for value in values]
        along_zx = jnp.concatenate([piece.astype(BF16) for piece in pieces], axis=0)
        acc[...] += lax.dot_general(along_y, along_zx, NT, preferred_element_type=F32)

    def take_part(part):
        def arrived(k):
            copy1(k).wait_recv()
        loop(
            jnp.maximum(part * part_slots, FIRST), jnp.minimum((part + 1) * part_slots, LAST), arrived
        )
        first = pl.multiple_of(part * part_rows, TILE)
        turned = lax.dot_general(
            small[0 : groups * TILE], recv1[pl.ds(first, part_rows)], NT, preferred_element_type=F32
        )
        send2[part] = turned.astype(BF16)
        loop(1, groups, lambda e: copy2(part, e).start())
        recv2[part, :, 0:part_rows] = send2[part, pl.ds(pl.multiple_of(my_group * TILE, TILE), TILE)]

    def grid_part(part):
        loop(1, groups, lambda e: copy2(part, e).wait_recv())
        loop(0, groups * part_rows // step, functools.partial(spread_part, part))

    def pipeline(part):
        take_part(part)
        grid_part(part - 1)

    fetches[5].wait()
    take_part(0)
    loop(1, parts, pipeline)
    grid_part(parts - 1)

    fetches[6].wait()
    lane = lax.broadcasted_iota(jnp.int32, (ny, LANES), 1)
    low, high = acc[:half, :LANES], acc[:half, LANES:]
    low_rim, high_rim = acc[half:, :LANES], acc[half:, LANES:]
    grid = jnp.concatenate(
        [low[:TILE] + high_rim, low[TILE:], high[:TILE] + low_rim, high[TILE:]], axis=0
    )
    other = jnp.where(
        (lane // TILE) % 2 == 0, -pltpu.roll(grid, LANES - TILE, 1), pltpu.roll(grid, TILE, 1)
    )
    both = jnp.concatenate([grid, other], axis=0)
    both_high = both.astype(BF16)
    both_low = (both - both_high.astype(F32)).astype(BF16)
    both_bits = jnp.concatenate([both_high, both_low], axis=1)
    wide = jnp.dot(table[0], both_bits, preferred_element_type=F32)
    turned = wide[:, :LANES] + wide[:, LANES:]
    turned = turned + jnp.dot(table[1], both_high, preferred_element_type=F32)
    send3[...] = turned.astype(BF16)

    mine3 = gz % nz * nx_hi + gz // nz
    others(0, n_gz, mine3, lambda index: copy3(index).start())
    here = pl.ds(pl.multiple_of(gz * TILE, TILE), TILE)
    recv3[here] = send3[here]
    others(0, n_gz, gz, lambda peer: arrival3(peer).wait_recv())

    got = recv3[...]
    past = jnp.dot(got, small[groups * TILE :], preferred_element_type=F32)
    planes = got.astype(F32) + jnp.concatenate([past[-TILE:], past[:-TILE]], axis=0)
    per = LANES // TILE
    spot = lax.broadcasted_iota(jnp.int32, (TILE, LANES), 1) // TILE
    ordered = []
    for s in range(2 * columns):
        across = []
        for t in range(n_gz // per):
            value = jnp.zeros((TILE, LANES), F32)
            for j in range(per):
                first = (t * per + j) * TILE
                tile = planes[first : first + TILE]
                turn = (j - s) * TILE % LANES
                tile = pltpu.roll(tile, turn, 1) if turn else tile
                value = jnp.where(spot == j, tile, value)
            across.append(value.astype(BF16))
        ordered.append(jnp.concatenate(across, axis=1))
    ordered = jnp.concatenate(ordered, axis=0)
    volume = jnp.dot(ordered, table[0], preferred_element_type=F32)
    volume = volume + jnp.dot(ordered, table[1], preferred_element_type=F32)
    for x in range(columns):
        real = volume[2 * x * TILE : (2 * x + 1) * TILE]
        imag = volume[(2 * x + 1) * TILE : (2 * x + 2) * TILE]
        out_ref[0, x] = real[:, :ny] - imag[:, ny:]
        out_ref[1, x] = real[:, ny:] + imag[:, :ny]

    loop(FIRST, LAST, lambda k: copy1(k).wait_send())
    loop(0, parts, lambda part: loop(1, groups, lambda e: copy2(part, e).wait_send()))
    others(0, n_gz, mine3, lambda index: copy3(index).wait_send())


def local(sizes, pixels, taps, plane_offset, grid_row, slab_of_block):
    n_img, n_gz, n_gy, width, ny, parts, step = sizes
    groups = n_img * n_gy
    columns = width // groups
    rows = pixels.shape[2]
    slots = n_gz * CAPACITY * TILE
    vmem = pl.BlockSpec(memory_space=pltpu.VMEM)
    return pl.pallas_call(
        functools.partial(kernel, sizes),
        out_shape=jax.ShapeDtypeStruct((2, columns, ny // n_gz, ny), F32),
        in_specs=[pl.BlockSpec(memory_space=pl.ANY)] * 7,
        out_specs=vmem,
        scratch_shapes=[
            pltpu.VMEM((2, width, rows), BF16),
            pltpu.VMEM((taps.shape[0], rows), BF16),
            pltpu.VMEM((rows,), jnp.int32),
            pltpu.VMEM((rows,), jnp.int32),
            pltpu.VMEM((1, rows // TILE), jnp.int32),
            pltpu.VMEM((groups * TILE + LANES, LANES), BF16),
            pltpu.VMEM((LANES, rows), BF16),
            pltpu.VMEM((slots, LANES), BF16),
            pltpu.VMEM((slots, LANES), BF16),
            pltpu.VMEM((parts, groups * TILE, slots // parts), BF16),
            pltpu.VMEM((parts, TILE, groups * slots // parts), BF16),
            pltpu.VMEM((ny // 2 + TILE, 2 * LANES), F32),
            pltpu.VMEM((2, ny, 2 * ny), BF16),
            pltpu.VMEM((ny, LANES), BF16),
            pltpu.VMEM((ny, LANES), BF16),
            pltpu.SemaphoreType.DMA((n_gz,)),
            pltpu.SemaphoreType.DMA((n_gz,)),
            pltpu.SemaphoreType.DMA((parts, groups)),
            pltpu.SemaphoreType.DMA((parts, groups)),
            pltpu.SemaphoreType.DMA((n_gz,)),
            pltpu.SemaphoreType.DMA((n_gz,)),
            pltpu.SemaphoreType.DMA((7,)),
        ],
        compiler_params=pltpu.CompilerParams(
            collective_id=0, has_side_effects=True, vmem_limit_bytes=64 * 1024 * 1024
        ),
    )(
        pixels, taps, plane_offset, grid_row, slab_of_block.reshape(1, rows // TILE),
        jnp.asarray(np.concatenate([pick_table(width, groups), rim_table(columns)])),
        jnp.asarray(transform_table(ny)),
    )


def solution(mesh, width=48, ny=512, parts=4, step=3072):
    sizes = (mesh.shape["img"], mesh.shape["gz"], mesh.shape["gy"], width, ny, parts, step)
    return jax.shard_map(
        functools.partial(local, sizes),
        mesh=mesh,
        in_specs=(
            P(None, None, ("img", "gz", "gy")),
            P(None, ("img", "gz", "gy")),
            P(("img", "gz", "gy")),
            P(("img", "gz", "gy")),
            P(("img", "gz", "gy"), None),
        ),
        out_specs=P(None, ("img", "gy"), "gz", None),
        check_vma=False,
    )
```

```python
import functools
import math

import jax
import jax.numpy as jnp
import numpy as np
from jax import lax
from jax.experimental import pallas as pl
from jax.experimental.pallas import tpu as pltpu
from jax.sharding import PartitionSpec as P

MESH = pl.DeviceIdType.MESH
F32 = jnp.float32
BF16 = jnp.bfloat16
TILE = 16
CAPACITY = 3
META = 8
LANES = 128
NT = (((1,), (1,)), ((), ()))


def transform_table(length):
    steps = np.arange(length)
    phase = (steps[:, None] * steps[None, :] % length) * (2.0 * math.pi / length)
    table = np.concatenate([np.cos(phase), np.sin(phase)], axis=1) / math.sqrt(length)
    table = table.astype(np.float32)
    high = table.astype(jnp.bfloat16)
    low = (table - high.astype(np.float32)).astype(jnp.bfloat16)
    return np.stack([high, low])


def pick_table(width, groups):
    columns = width // groups
    pick = np.zeros((groups, TILE, LANES), np.float32)
    for group in range(groups):
        for s in range(2 * columns):
            pick[group, s, (s % 2) * width + group * columns + s // 2] = 1.0
        for s in range(META):
            pick[group, 2 * columns + s, 2 * width + s] = 1.0
    return pick.reshape(groups * TILE, LANES).astype(jnp.bfloat16)


def rim_table(columns):
    place = np.zeros((LANES, LANES), np.float32)
    for x in range(columns):
        for c in range(2):
            for z in range(2):
                place[2 * columns * TILE + TILE * c + 2 * x + z, (2 * x + c) * TILE + z] = 1.0
    return place.astype(jnp.bfloat16)


def kernel(
    sizes, pix_hbm, taps_hbm, plane_hbm, row_hbm, slab_hbm, small_hbm, table_hbm, out_ref,
    pix_ref, taps_ref, plane_ref, row_ref, slab_ref, small, x_buf, send1, recv1, send2, recv2, acc, table, send3, recv3,
    s1_sem, r1_sem, s2_sem, r2_sem, s3_sem, r3_sem, in_sem,
):
    n_img, n_gz, n_gy, width, ny, parts, step = sizes
    nx_hi = 2
    nz = n_gz // nx_hi
    groups = n_img * n_gy
    columns = width // groups
    rows = pix_hbm.shape[2]
    blocks = rows // TILE
    slot_rows = CAPACITY * TILE
    part_slots = n_gz // parts
    part_rows = part_slots * slot_rows
    half = ny // 2
    reach = nz // 2
    sends = n_gz // 2
    own_send = sends - nx_hi

    img, gz, gy = lax.axis_index("img"), lax.axis_index("gz"), lax.axis_index("gy")
    my_group = img * n_gy + gy

    my_x, my_z = lax.div(gz, nz), lax.rem(gz, nz)
    my_y, my_side = lax.div(img, 2), lax.rem(img, 2)

    def slab_peer(k):
        turn, m = k % sends % nx_hi, k % sends // nx_hi
        x = lax.rem(my_x + turn, nx_hi)
        along = (reach - m) // 2 * (2 * (m % 2) - 1) + nz
        z = my_z + along + (x * reach if m == 0 else 0)
        return x * nz + lax.rem(z, nz)

    def any_peer(k):
        turn, m = k % nx_hi, nz - 1 - k // nx_hi
        along = (m + 1) // 2 * (2 * (m % 2) - 1) + nz
        return lax.rem(my_x + turn, nx_hi) * nz + lax.rem(my_z + along, nz)

    any_own = n_gz - nx_hi
    any_others = [k for k in range(n_gz) if k != any_own]

    def group_peer(e):
        core, side, along = e % n_gy, e // n_gy % 2, e // n_gy // 2
        y = lax.rem(my_y + along, n_img // 2)
        return y * 2 + lax.rem(my_side + side, 2), lax.rem(gy + core, n_gy)

    def copy1(k):
        peer = slab_peer(k)
        return pltpu.make_async_remote_copy(
            src_ref=send1.at[pl.ds(pl.multiple_of(k * slot_rows, TILE), slot_rows)],
            dst_ref=recv1.at[pl.ds(pl.multiple_of(k * slot_rows, TILE), slot_rows)],
            send_sem=s1_sem.at[0], recv_sem=r1_sem.at[k // part_slots],
            device_id=(img, peer, gy), device_id_type=MESH,
        )

    def copy2(part, e):
        to_img, to_gy = group_peer(e)
        peer = to_img * n_gy + to_gy
        return pltpu.make_async_remote_copy(
            src_ref=send2.at[part, pl.ds(pl.multiple_of(peer * TILE, TILE), TILE)],
            dst_ref=recv2.at[part, :, pl.ds(pl.multiple_of(e * part_rows, LANES), part_rows)],
            send_sem=s2_sem.at[0], recv_sem=r2_sem.at[part],
            device_id=(to_img, gz, to_gy), device_id_type=MESH,
        )

    def copy3(slab, k):
        peer = any_peer(k)
        return pltpu.make_async_remote_copy(
            src_ref=send3.at[slab, pl.ds(pl.multiple_of(peer * TILE, TILE), TILE)],
            dst_ref=recv3.at[slab, pl.ds(pl.multiple_of(gz * TILE, TILE), TILE)],
            send_sem=s3_sem.at[0], recv_sem=r3_sem.at[slab],
            device_id=(img, peer, gy), device_id_type=MESH,
        )

    pairs = [
        (slab_hbm, slab_ref), (taps_hbm, taps_ref), (plane_hbm, plane_ref), (row_hbm, row_ref),
        (pix_hbm, pix_ref), (small_hbm, small), (table_hbm, table),
    ]
    fetches = [pltpu.make_async_copy(*pair, in_sem.at[i]) for i, pair in enumerate(pairs)]
    for fetch in fetches:
        fetch.start()

    def landed(view, sem):
        pltpu.make_async_remote_copy(
            src_ref=view, dst_ref=view, send_sem=s1_sem.at[0], recv_sem=sem,
            device_id=(img, any_peer(0), gy), device_id_type=MESH,
        ).wait_recv()

    def left(view, sem):
        pltpu.make_async_remote_copy(
            src_ref=view, dst_ref=view, send_sem=sem, recv_sem=r1_sem.at[0],
            device_id=(img, any_peer(0), gy), device_id_type=MESH,
        ).wait_send()

    def loop(first, last, do):
        def body(index, carry):
            do(index)
            return carry
        lax.fori_loop(first, last, body, 0)

    barrier = pltpu.get_barrier_semaphore()

    for k in any_others:
        pl.semaphore_signal(
            barrier, inc=1, device_id=(img, any_peer(k), gy), device_id_type=MESH
        )
    for e in range(1, groups):
        to_img, to_gy = group_peer(e)
        pl.semaphore_signal(barrier, inc=1, device_id=(to_img, gz, to_gy), device_id_type=MESH)

    for fetch in fetches[:5]:
        fetch.wait()
    taps = taps_ref[...].astype(F32)
    x_iota = lax.broadcasted_iota(jnp.int32, (width, rows), 0)
    for c in range(2):
        p = pix_ref[c].astype(F32)
        before = jnp.where(x_iota == 0, 0.0, pltpu.roll(p, 1, 0))
        after = jnp.where(x_iota == width - 1, 0.0, pltpu.roll(p, width - 1, 0))
        spread = taps[6:7] * before + taps[7:8] * p + taps[8:9] * after
        x_buf[c * width : (c + 1) * width] = spread.astype(BF16)
    data = jnp.concatenate(
        [
            taps[0:6], plane_ref[...].reshape(1, rows).astype(F32),
            (row_ref[...].reshape(1, rows) - half).astype(F32),
            jnp.zeros((LANES - 2 * width - META, rows), F32),
        ],
        axis=0,
    )
    x_buf[2 * width :] = data.astype(BF16)

    block_iota = lax.broadcasted_iota(jnp.int32, (blocks, rows), 0)
    row_iota = lax.broadcasted_iota(jnp.int32, (blocks, rows), 1)
    row_block = row_iota // TILE
    square = (blocks, blocks)
    diagonal = lax.broadcasted_iota(jnp.int32, square, 0) == lax.broadcasted_iota(jnp.int32, square, 1)
    target = jnp.sum(jnp.where(diagonal, slab_ref[...], 0), axis=1, keepdims=True)
    target = jnp.broadcast_to(target, (blocks, rows))
    own = jnp.sum(jnp.where(block_iota == row_block, target, 0), axis=0, keepdims=True)
    earlier = jnp.where((target == own) & (block_iota < row_block), 1, 0)
    rank = jnp.sum(earlier, axis=0, keepdims=True)
    side = own // nz
    turn = (side - gz // nz + nx_hi) % nx_hi
    along = (own % nz - gz % nz + nz + reach // 2 - side + nz) % nz
    far_owner = along // reach
    along = along % reach - reach // 2 + side
    order = jnp.where(along >= 0, jnp.maximum(reach - 1 - 2 * along, 0), reach + 2 * along)
    order = far_owner * sends + order * nx_hi + turn
    place = (order * CAPACITY + rank) * TILE + row_iota[0:1] % TILE

    slot_iota = lax.broadcasted_iota(jnp.int32, (part_rows, rows), 0)
    pl.semaphore_wait(barrier, n_gz + groups - 2)

    def part_sends(part):
        every = range(part * part_slots, (part + 1) * part_slots)
        return [k for k in every if k % sends != own_send]

    def permute(index):
        first = index * part_rows
        chosen = jnp.where(slot_iota == place - first, 1.0, 0.0).astype(BF16)
        moved = lax.dot_general(chosen, x_buf[...], NT, preferred_element_type=F32)
        send1[first : first + part_rows] = moved.astype(BF16)
        for k in part_sends(index):
            copy1(k).start()

    for part in range(parts):
        permute(part)
    for k in (own_send, own_send + sends):
        recv1[k * slot_rows : (k + 1) * slot_rows] = send1[k * slot_rows : (k + 1) * slot_rows]

    acc[...] = jnp.zeros_like(acc)
    y_iota = (lax.broadcasted_iota(jnp.int32, (half + TILE, step), 0) - half // 2).astype(BF16)
    z_iota = lax.broadcasted_iota(jnp.int32, (TILE, step), 0)
    rim_x = z_iota // 2
    rim_z = (z_iota % 2 + TILE).astype(BF16)
    z_iota = z_iota.astype(BF16)

    def spread_part(part, index):
        got = recv2[part, :, pl.ds(pl.multiple_of(index * step, step), step)]
        zero = jnp.zeros((), BF16)
        y = got[13:14].astype(F32) + (half - 1.0)
        y = jnp.where(y < 0.0, y + ny, y)
        upper = y >= half
        y = jnp.where(upper, y - half, y) - half // 2
        ys = [(y + b).astype(BF16) for b in range(3)]
        in_high = jnp.where(upper, 1.0, 0.0).astype(BF16)
        got = got.astype(BF16)
        z0 = got[12:13]
        z1, z2 = z0 + 1, z0 + 2
        along_y = jnp.where(
            y_iota == ys[0], got[9:10],
            jnp.where(y_iota == ys[1], got[10:11], jnp.where(y_iota == ys[2], got[11:12], zero)),
        ).astype(BF16)
        along_z = jnp.where(
            z_iota == z0, got[6:7],
            jnp.where(z_iota == z1, got[7:8], jnp.where(z_iota == z2, got[8:9], zero)),
        )
        rim = jnp.where(rim_z == z1, got[7:8], jnp.where(rim_z == z2, got[8:9], zero))
        values = []
        for c in range(2):
            value = jnp.zeros((TILE, step), BF16)
            for x in range(columns):
                value = jnp.where(rim_x == x, got[2 * x + c : 2 * x + c + 1], value)
            values.append(value)
        pieces = []
        for mask in (1 - in_high, in_high):
            z_part, rim_part = along_z * mask, rim * mask
            pieces += [z_part * got[s : s + 1] for s in range(2 * columns)]
            pieces += [rim_part * value for value in values]
        along_zx = jnp.concatenate([piece.astype(BF16) for piece in pieces], axis=0)
        acc[part // (parts // 2)] += lax.dot_general(along_y, along_zx, NT, preferred_element_type=F32)

    def take_part(part):
        landed(recv1.at[pl.ds(0, len(part_sends(part)) * slot_rows)], r1_sem.at[part])
        first = part * part_rows
        turned = lax.dot_general(
            small[0 : groups * TILE], recv1[first : first + part_rows], NT, preferred_element_type=F32
        )
        send2[part] = turned.astype(BF16)
        for e in range(1, groups):
            copy2(part, e).start()
        recv2[part, :, 0:part_rows] = send2[part, pl.ds(pl.multiple_of(my_group * TILE, TILE), TILE)]

    def grid_part(part):
        landed(recv2.at[part, :, pl.ds(0, (groups - 1) * part_rows)], r2_sem.at[part])
        loop(0, groups * part_rows // step, functools.partial(spread_part, part))

    lane = lax.broadcasted_iota(jnp.int32, (ny, LANES), 1)
    here = pl.ds(pl.multiple_of(gz * TILE, TILE), TILE)

    def turn_y(slab):
        low, high = acc[slab, :half, :LANES], acc[slab, :half, LANES:]
        low_rim, high_rim = acc[slab, half:, :LANES], acc[slab, half:, LANES:]
        grid = jnp.concatenate(
            [low[:TILE] + high_rim, low[TILE:], high[:TILE] + low_rim, high[TILE:]], axis=0
        )
        other = jnp.where(
            (lane // TILE) % 2 == 0, -pltpu.roll(grid, LANES - TILE, 1), pltpu.roll(grid, TILE, 1)
        )
        both = jnp.concatenate([grid, other], axis=0)
        both_high = both.astype(BF16)
        both_low = (both - both_high.astype(F32)).astype(BF16)
        both_bits = jnp.concatenate([both_high, both_low], axis=1)
        wide = jnp.dot(table[0], both_bits, preferred_element_type=F32)
        turned = wide[:, :LANES] + wide[:, LANES:]
        turned = turned + jnp.dot(table[1], both_high, preferred_element_type=F32)
        send3[slab] = turned.astype(BF16)
        for k in any_others:
            copy3(slab, k).start()
        recv3[slab, here] = send3[slab, here]

    fetches[5].wait()
    fetches[6].wait()
    per_slab = parts // 2
    for part in range(parts):
        take_part(part)

    def slab_step(slab):
        grid_part(slab * per_slab)

        loop(slab * per_slab + 1, (slab + 1) * per_slab, grid_part)
        turn_y(slab)

    loop(0, 2, slab_step)
    left(send1.at[pl.ds(0, (n_gz - 2) * slot_rows)], s1_sem.at[0])
    left(recv2.at[:, :, pl.ds(0, (groups - 1) * part_rows)], s2_sem.at[0])
    for slab in range(2):
        landed(recv3.at[slab, pl.ds(0, (n_gz - 1) * TILE)], r3_sem.at[slab])
    left(recv3.at[:, pl.ds(0, (n_gz - 1) * TILE)], s3_sem.at[0])

    got = recv3[0]
    span = reach * TILE
    swapped = [recv3[1, (2 * x + 1 - i) * span : (2 * x + 2 - i) * span] for x in range(nx_hi) for i in range(2)]
    swapped = jnp.concatenate(swapped, axis=0)
    place_rim = small[groups * TILE :]
    past = jnp.dot(got, place_rim, preferred_element_type=F32)
    past = past + jnp.dot(swapped, place_rim, preferred_element_type=F32)
    planes = got.astype(F32) + swapped.astype(F32) + jnp.concatenate([past[-TILE:], past[:-TILE]], axis=0)
    per = LANES // TILE
    spot = lax.broadcasted_iota(jnp.int32, (TILE, LANES), 1) // TILE
    ordered = []
    for s in range(2 * columns):
        across = []
        for t in range(n_gz // per):
            value = jnp.zeros((TILE, LANES), F32)
            for j in range(per):
                first = (t * per + j) * TILE
                tile = planes[first : first + TILE]
                turn = (j - s) * TILE % LANES
                tile = pltpu.roll(tile, turn, 1) if turn else tile
                value = jnp.where(spot == j, tile, value)
            across.append(value)
        ordered.append(jnp.concatenate(across, axis=1))
    ordered = jnp.concatenate(ordered, axis=0)
    ordered_high = ordered.astype(BF16)
    ordered_low = (ordered - ordered_high.astype(F32)).astype(BF16)
    ordered_bits = jnp.concatenate([ordered_high, ordered_low], axis=0)
    lines = ordered.shape[0]
    wide = jnp.dot(ordered_bits, table[0], preferred_element_type=F32)
    volume = wide[:lines] + wide[lines:]
    volume = volume + jnp.dot(ordered_high, table[1], preferred_element_type=F32)
    for x in range(columns):
        real = volume[2 * x * TILE : (2 * x + 1) * TILE]
        imag = volume[(2 * x + 1) * TILE : (2 * x + 2) * TILE]
        out_ref[0, x] = real[:, :ny] - imag[:, ny:]
        out_ref[1, x] = real[:, ny:] + imag[:, :ny]


def local(sizes, pixels, taps, plane_offset, grid_row, slab_of_block):
    n_img, n_gz, n_gy, width, ny, parts, step = sizes
    groups = n_img * n_gy
    columns = width // groups
    rows = pixels.shape[2]
    slots = n_gz * CAPACITY * TILE
    vmem = pl.BlockSpec(memory_space=pltpu.VMEM)
    return pl.pallas_call(
        functools.partial(kernel, sizes),
        out_shape=jax.ShapeDtypeStruct((2, columns, ny // n_gz, ny), F32),
        in_specs=[pl.BlockSpec(memory_space=pl.ANY)] * 7,
        out_specs=vmem,
        scratch_shapes=[
            pltpu.VMEM((2, width, rows), BF16),
            pltpu.VMEM((taps.shape[0], rows), BF16),
            pltpu.VMEM((rows,), jnp.int32),
            pltpu.VMEM((rows,), jnp.int32),
            pltpu.VMEM((1, rows // TILE), jnp.int32),
            pltpu.VMEM((groups * TILE + LANES, LANES), BF16),
            pltpu.VMEM((LANES, rows), BF16),
            pltpu.VMEM((slots, LANES), BF16),
            pltpu.VMEM((slots, LANES), BF16),
            pltpu.VMEM((parts, groups * TILE, slots // parts), BF16),
            pltpu.VMEM((parts, TILE, groups * slots // parts), BF16),
            pltpu.VMEM((2, ny // 2 + TILE, 2 * LANES), F32),
            pltpu.VMEM((2, ny, 2 * ny), BF16),
            pltpu.VMEM((2, ny, LANES), BF16),
            pltpu.VMEM((2, ny, LANES), BF16),
            pltpu.SemaphoreType.DMA((1,)),
            pltpu.SemaphoreType.DMA((parts,)),
            pltpu.SemaphoreType.DMA((1,)),
            pltpu.SemaphoreType.DMA((parts,)),
            pltpu.SemaphoreType.DMA((1,)),
            pltpu.SemaphoreType.DMA((2,)),
            pltpu.SemaphoreType.DMA((7,)),
        ],
        compiler_params=pltpu.CompilerParams(
            collective_id=0, has_side_effects=True, vmem_limit_bytes=64 * 1024 * 1024
        ),
    )(
        pixels, taps, plane_offset, grid_row, slab_of_block.reshape(1, rows // TILE),
        jnp.asarray(np.concatenate([pick_table(width, groups), rim_table(columns)])),
        jnp.asarray(transform_table(ny)),
    )


def solution(mesh, width=48, ny=512, parts=4, step=3072):
    sizes = (mesh.shape["img"], mesh.shape["gz"], mesh.shape["gy"], width, ny, parts, step)
    return jax.shard_map(
        functools.partial(local, sizes),
        mesh=mesh,
        in_specs=(
            P(None, None, ("img", "gz", "gy")),
            P(None, ("img", "gz", "gy")),
            P(("img", "gz", "gy")),
            P(("img", "gz", "gy")),
            P(("img", "gz", "gy"), None),
        ),
        out_specs=P(None, ("img", "gy"), "gz", None),
        check_vma=False,
    )
```

```python
import functools
import math

import jax
import jax.numpy as jnp
import numpy as np
from jax import lax
from jax.experimental import pallas as pl
from jax.experimental.pallas import tpu as pltpu
from jax.sharding import PartitionSpec as P

MESH = pl.DeviceIdType.MESH
F32 = jnp.float32
BF16 = jnp.bfloat16
TILE = 16
CAPACITY = 3
META = 8
LANES = 128
NT = (((1,), (1,)), ((), ()))


def transform_table(length):
    steps = np.arange(length)
    phase = (steps[:, None] * steps[None, :] % length) * (2.0 * math.pi / length)
    table = np.concatenate([np.cos(phase), np.sin(phase)], axis=1) / math.sqrt(length)
    table = table.astype(np.float32)
    high = table.astype(jnp.bfloat16)
    low = (table - high.astype(np.float32)).astype(jnp.bfloat16)
    return np.stack([high, low])


def pick_table(width, groups):
    columns = width // groups
    pick = np.zeros((groups, TILE, LANES), np.float32)
    for group in range(groups):
        for s in range(2 * columns):
            pick[group, s, (s % 2) * width + group * columns + s // 2] = 1.0
        for s in range(META):
            pick[group, 2 * columns + s, 2 * width + s] = 1.0
    return pick.reshape(groups * TILE, LANES).astype(jnp.bfloat16)


def rim_table(columns):
    place = np.zeros((LANES, LANES), np.float32)
    for x in range(columns):
        for c in range(2):
            for z in range(2):
                place[2 * columns * TILE + TILE * c + 2 * x + z, (2 * x + c) * TILE + z] = 1.0
    return place.astype(jnp.bfloat16)


def kernel(
    sizes, pix_hbm, taps_hbm, plane_hbm, row_hbm, slab_hbm, small_hbm, table_hbm, out_ref,
    pix_ref, taps_ref, plane_ref, row_ref, slab_ref, small, x_buf, send1, recv1, send2, recv2, acc, table, send3, recv3,
    s1_sem, r1_sem, s2_sem, r2_sem, s3_sem, r3_sem, in_sem,
):
    n_img, n_gz, n_gy, width, ny, parts, step = sizes
    nx_hi = 2
    nz = n_gz // nx_hi
    groups = n_img * n_gy
    columns = width // groups
    rows = pix_hbm.shape[2]
    blocks = rows // TILE
    slot_rows = CAPACITY * TILE
    part_slots = n_gz // parts
    part_rows = part_slots * slot_rows
    half = ny // 2
    reach = nz // 2
    sends = n_gz // 2
    own_send = sends - nx_hi

    img, gz, gy = lax.axis_index("img"), lax.axis_index("gz"), lax.axis_index("gy")
    my_group = img * n_gy + gy

    my_x, my_z = lax.div(gz, nz), lax.rem(gz, nz)
    my_y, my_side = lax.div(img, 2), lax.rem(img, 2)

    def slab_peer(k):
        turn, m = k % sends % nx_hi, k % sends // nx_hi
        x = lax.rem(my_x + turn, nx_hi)
        along = (reach - m) // 2 * (2 * (m % 2) - 1) + nz
        z = my_z + along + (x * reach if m == 0 else 0)
        return x * nz + lax.rem(z, nz)

    def any_peer(k):
        turn, m = k % nx_hi, nz - 1 - k // nx_hi
        along = (m + 1) // 2 * (2 * (m % 2) - 1) + nz
        return lax.rem(my_x + turn, nx_hi) * nz + lax.rem(my_z + along, nz)

    any_own = n_gz - nx_hi
    any_others = [k for k in range(n_gz) if k != any_own]

    def group_peer(e):
        core, side, along = e % n_gy, e // n_gy % 2, e // n_gy // 2
        y = lax.rem(my_y + along, n_img // 2)
        return y * 2 + lax.rem(my_side + side, 2), lax.rem(gy + core, n_gy)

    def copy1(k):
        peer = slab_peer(k)
        return pltpu.make_async_remote_copy(
            src_ref=send1.at[pl.ds(pl.multiple_of(k * slot_rows, TILE), slot_rows)],
            dst_ref=recv1.at[pl.ds(pl.multiple_of(k * slot_rows, TILE), slot_rows)],
            send_sem=s1_sem.at[0], recv_sem=r1_sem.at[k // part_slots],
            device_id=(img, peer, gy), device_id_type=MESH,
        )

    def copy2(part, e):
        to_img, to_gy = group_peer(e)
        peer = to_img * n_gy + to_gy
        return pltpu.make_async_remote_copy(
            src_ref=send2.at[part, pl.ds(pl.multiple_of(peer * TILE, TILE), TILE)],
            dst_ref=recv2.at[part, :, pl.ds(pl.multiple_of(e * part_rows, LANES), part_rows)],
            send_sem=s2_sem.at[0], recv_sem=r2_sem.at[part],
            device_id=(to_img, gz, to_gy), device_id_type=MESH,
        )

    def copy3(slab, peer):
        return pltpu.make_async_remote_copy(
            src_ref=send3.at[slab, pl.ds(pl.multiple_of(peer * TILE, TILE), TILE)],
            dst_ref=recv3.at[slab, pl.ds(pl.multiple_of(gz * TILE, TILE), TILE)],
            send_sem=s3_sem.at[0], recv_sem=r3_sem.at[slab],
            device_id=(img, peer, gy), device_id_type=MESH,
        )

    pairs = [
        (slab_hbm, slab_ref), (taps_hbm, taps_ref), (plane_hbm, plane_ref), (row_hbm, row_ref),
        (pix_hbm, pix_ref), (small_hbm, small), (table_hbm, table),
    ]
    fetches = [pltpu.make_async_copy(*pair, in_sem.at[i]) for i, pair in enumerate(pairs)]
    for fetch in fetches:
        fetch.start()

    def landed(view, sem):
        pltpu.make_async_remote_copy(
            src_ref=view, dst_ref=view, send_sem=s1_sem.at[0], recv_sem=sem,
            device_id=(img, any_peer(0), gy), device_id_type=MESH,
        ).wait_recv()

    def left(view, sem):
        pltpu.make_async_remote_copy(
            src_ref=view, dst_ref=view, send_sem=sem, recv_sem=r1_sem.at[0],
            device_id=(img, any_peer(0), gy), device_id_type=MESH,
        ).wait_send()

    def loop(first, last, do):
        def body(index, carry):
            do(index)
            return carry
        lax.fori_loop(first, last, body, 0)

    barrier = pltpu.get_barrier_semaphore()

    near = [k for k in any_others if nz - 1 - k // nx_hi <= reach]
    for k in near:
        pl.semaphore_signal(
            barrier, inc=1, device_id=(img, any_peer(k), gy), device_id_type=MESH
        )
    for e in range(1, groups):
        to_img, to_gy = group_peer(e)
        pl.semaphore_signal(barrier, inc=1, device_id=(to_img, gz, to_gy), device_id_type=MESH)

    for fetch in fetches[:5]:
        fetch.wait()
    taps = taps_ref[...].astype(F32)
    x_iota = lax.broadcasted_iota(jnp.int32, (width, rows), 0)
    for c in range(2):
        p = pix_ref[c].astype(F32)
        before = jnp.where(x_iota == 0, 0.0, pltpu.roll(p, 1, 0))
        after = jnp.where(x_iota == width - 1, 0.0, pltpu.roll(p, width - 1, 0))
        spread = taps[6:7] * before + taps[7:8] * p + taps[8:9] * after
        x_buf[c * width : (c + 1) * width] = spread.astype(BF16)
    data = jnp.concatenate(
        [
            taps[0:6], plane_ref[...].reshape(1, rows).astype(F32),
            (row_ref[...].reshape(1, rows) - half).astype(F32),
            jnp.zeros((LANES - 2 * width - META, rows), F32),
        ],
        axis=0,
    )
    x_buf[2 * width :] = data.astype(BF16)

    block_iota = lax.broadcasted_iota(jnp.int32, (blocks, rows), 0)
    row_iota = lax.broadcasted_iota(jnp.int32, (blocks, rows), 1)
    row_block = row_iota // TILE
    square = (blocks, blocks)
    diagonal = lax.broadcasted_iota(jnp.int32, square, 0) == lax.broadcasted_iota(jnp.int32, square, 1)
    target = jnp.sum(jnp.where(diagonal, slab_ref[...], 0), axis=1, keepdims=True)
    target = jnp.broadcast_to(target, (blocks, rows))
    own = jnp.sum(jnp.where(block_iota == row_block, target, 0), axis=0, keepdims=True)
    earlier = jnp.where((target == own) & (block_iota < row_block), 1, 0)
    rank = jnp.sum(earlier, axis=0, keepdims=True)
    side = own // nz
    turn = (side - gz // nz + nx_hi) % nx_hi
    along = (own % nz - gz % nz + nz + reach // 2 - side + nz) % nz
    far_owner = along // reach
    along = along % reach - reach // 2 + side
    order = jnp.where(along >= 0, jnp.maximum(reach - 1 - 2 * along, 0), reach + 2 * along)
    order = far_owner * sends + order * nx_hi + turn
    place = (order * CAPACITY + rank) * TILE + row_iota[0:1] % TILE

    slot_iota = lax.broadcasted_iota(jnp.int32, (part_rows, rows), 0)
    pl.semaphore_wait(barrier, len(near) + groups - 1)

    def part_sends(part):
        every = range(part * part_slots, (part + 1) * part_slots)
        return [k for k in every if k % sends != own_send]

    def permute(index):
        first = index * part_rows
        chosen = jnp.where(slot_iota == place - first, 1.0, 0.0).astype(BF16)
        moved = lax.dot_general(chosen, x_buf[...], NT, preferred_element_type=F32)
        send1[first : first + part_rows] = moved.astype(BF16)
        for k in part_sends(index):
            copy1(k).start()

    for part in range(parts):
        permute(part)
    for k in (own_send, own_send + sends):
        recv1[k * slot_rows : (k + 1) * slot_rows] = send1[k * slot_rows : (k + 1) * slot_rows]

    acc[...] = jnp.zeros_like(acc)
    y_iota = (lax.broadcasted_iota(jnp.int32, (half + TILE, step), 0) - half // 2).astype(BF16)
    z_iota = lax.broadcasted_iota(jnp.int32, (TILE, step), 0)
    rim_x = z_iota // 2
    rim_z = (z_iota % 2 + TILE).astype(BF16)
    z_iota = z_iota.astype(BF16)

    def spread_part(part, index):
        got = recv2[part, :, pl.ds(pl.multiple_of(index * step, step), step)]
        zero = jnp.zeros((), BF16)
        y = got[13:14].astype(F32) + (half - 1.0)
        y = jnp.where(y < 0.0, y + ny, y)
        upper = y >= half
        y = jnp.where(upper, y - half, y) - half // 2
        ys = [(y + b).astype(BF16) for b in range(3)]
        in_high = jnp.where(upper, 1.0, 0.0).astype(BF16)
        got = got.astype(BF16)
        z0 = got[12:13]
        z1, z2 = z0 + 1, z0 + 2
        along_y = jnp.where(
            y_iota == ys[0], got[9:10],
            jnp.where(y_iota == ys[1], got[10:11], jnp.where(y_iota == ys[2], got[11:12], zero)),
        ).astype(BF16)
        along_z = jnp.where(
            z_iota == z0, got[6:7],
            jnp.where(z_iota == z1, got[7:8], jnp.where(z_iota == z2, got[8:9], zero)),
        )
        rim = jnp.where(rim_z == z1, got[7:8], jnp.where(rim_z == z2, got[8:9], zero))
        values = []
        for c in range(2):
            value = jnp.zeros((TILE, step), BF16)
            for x in range(columns):
                value = jnp.where(rim_x == x, got[2 * x + c : 2 * x + c + 1], value)
            values.append(value)
        pieces = []
        for mask in (1 - in_high, in_high):
            z_part, rim_part = along_z * mask, rim * mask
            pieces += [z_part * got[s : s + 1] for s in range(2 * columns)]
            pieces += [rim_part * value for value in values]
        along_zx = jnp.concatenate([piece.astype(BF16) for piece in pieces], axis=0)
        acc[part // (parts // 2)] += lax.dot_general(along_y, along_zx, NT, preferred_element_type=F32)

    def take_part(part):
        landed(recv1.at[pl.ds(0, len(part_sends(part)) * slot_rows)], r1_sem.at[part])
        first = part * part_rows
        turned = lax.dot_general(
            small[0 : groups * TILE], recv1[first : first + part_rows], NT, preferred_element_type=F32
        )
        send2[part] = turned.astype(BF16)
        for e in range(1, groups):
            copy2(part, e).start()
        recv2[part, :, 0:part_rows] = send2[part, pl.ds(pl.multiple_of(my_group * TILE, TILE), TILE)]

    def grid_part(part):
        landed(recv2.at[part, :, pl.ds(0, (groups - 1) * part_rows)], r2_sem.at[part])
        loop(0, groups * part_rows // step, functools.partial(spread_part, part))

    lane = lax.broadcasted_iota(jnp.int32, (ny, LANES), 1)
    here = pl.ds(pl.multiple_of(gz * TILE, TILE), TILE)

    def turn_y(slab):
        low, high = acc[slab, :half, :LANES], acc[slab, :half, LANES:]
        low_rim, high_rim = acc[slab, half:, :LANES], acc[slab, half:, LANES:]
        grid = jnp.concatenate(
            [low[:TILE] + high_rim, low[TILE:], high[:TILE] + low_rim, high[TILE:]], axis=0
        )
        other = jnp.where(
            (lane // TILE) % 2 == 0, -pltpu.roll(grid, LANES - TILE, 1), pltpu.roll(grid, TILE, 1)
        )
        both = jnp.concatenate([grid, other], axis=0)
        both_high = both.astype(BF16)
        both_low = (both - both_high.astype(F32)).astype(BF16)
        both_bits = jnp.concatenate([both_high, both_low], axis=1)
        wide = jnp.dot(table[0], both_bits, preferred_element_type=F32)
        turned = wide[:, :LANES] + wide[:, LANES:]
        turned = turned + jnp.dot(table[1], both_high, preferred_element_type=F32)
        send3[slab] = turned.astype(BF16)
        for z in range(nz):
            for x in range(nx_hi):
                peer = x * nz + z

                @pl.when(gz != peer)
                def _():
                    copy3(slab, peer).start()
        recv3[slab, here] = send3[slab, here]

    fetches[5].wait()
    fetches[6].wait()
    per_slab = parts // 2
    for part in range(parts):
        take_part(part)

    def slab_step(slab):
        grid_part(slab * per_slab)

        loop(slab * per_slab + 1, (slab + 1) * per_slab, grid_part)
        turn_y(slab)

    loop(0, 2, slab_step)
    left(send1.at[pl.ds(0, (n_gz - 2) * slot_rows)], s1_sem.at[0])
    left(recv2.at[:, :, pl.ds(0, (groups - 1) * part_rows)], s2_sem.at[0])
    for slab in range(2):
        landed(recv3.at[slab, pl.ds(0, (n_gz - 1) * TILE)], r3_sem.at[slab])
    left(recv3.at[:, pl.ds(0, (n_gz - 1) * TILE)], s3_sem.at[0])

    got = recv3[0]
    span = reach * TILE
    swapped = [recv3[1, (2 * x + 1 - i) * span : (2 * x + 2 - i) * span] for x in range(nx_hi) for i in range(2)]
    swapped = jnp.concatenate(swapped, axis=0)
    place_rim = small[groups * TILE :]
    past = jnp.dot(got, place_rim, preferred_element_type=F32)
    past = past + jnp.dot(swapped, place_rim, preferred_element_type=F32)
    planes = got.astype(F32) + swapped.astype(F32) + jnp.concatenate([past[-TILE:], past[:-TILE]], axis=0)
    per = LANES // TILE
    spot = lax.broadcasted_iota(jnp.int32, (TILE, LANES), 1) // TILE
    ordered = []
    for s in range(2 * columns):
        across = []
        for t in range(n_gz // per):
            value = jnp.zeros((TILE, LANES), F32)
            for j in range(per):
                first = (t * per + j) * TILE
                tile = planes[first : first + TILE]
                turn = (j - s) * TILE % LANES
                tile = pltpu.roll(tile, turn, 1) if turn else tile
                value = jnp.where(spot == j, tile, value)
            across.append(value)
        ordered.append(jnp.concatenate(across, axis=1))
    ordered = jnp.concatenate(ordered, axis=0)
    ordered_high = ordered.astype(BF16)
    ordered_low = (ordered - ordered_high.astype(F32)).astype(BF16)
    ordered_bits = jnp.concatenate([ordered_high, ordered_low], axis=0)
    lines = ordered.shape[0]
    wide = jnp.dot(ordered_bits, table[0], preferred_element_type=F32)
    volume = wide[:lines] + wide[lines:]
    volume = volume + jnp.dot(ordered_high, table[1], preferred_element_type=F32)
    for x in range(columns):
        real = volume[2 * x * TILE : (2 * x + 1) * TILE]
        imag = volume[(2 * x + 1) * TILE : (2 * x + 2) * TILE]
        out_ref[0, x] = real[:, :ny] - imag[:, ny:]
        out_ref[1, x] = real[:, ny:] + imag[:, :ny]


def local(sizes, pixels, taps, plane_offset, grid_row, slab_of_block):
    n_img, n_gz, n_gy, width, ny, parts, step = sizes
    groups = n_img * n_gy
    columns = width // groups
    rows = pixels.shape[2]
    slots = n_gz * CAPACITY * TILE
    vmem = pl.BlockSpec(memory_space=pltpu.VMEM)
    return pl.pallas_call(
        functools.partial(kernel, sizes),
        out_shape=jax.ShapeDtypeStruct((2, columns, ny // n_gz, ny), F32),
        in_specs=[pl.BlockSpec(memory_space=pl.ANY)] * 7,
        out_specs=vmem,
        scratch_shapes=[
            pltpu.VMEM((2, width, rows), BF16),
            pltpu.VMEM((taps.shape[0], rows), BF16),
            pltpu.VMEM((rows,), jnp.int32),
            pltpu.VMEM((rows,), jnp.int32),
            pltpu.VMEM((1, rows // TILE), jnp.int32),
            pltpu.VMEM((groups * TILE + LANES, LANES), BF16),
            pltpu.VMEM((LANES, rows), BF16),
            pltpu.VMEM((slots, LANES), BF16),
            pltpu.VMEM((slots, LANES), BF16),
            pltpu.VMEM((parts, groups * TILE, slots // parts), BF16),
            pltpu.VMEM((parts, TILE, groups * slots // parts), BF16),
            pltpu.VMEM((2, ny // 2 + TILE, 2 * LANES), F32),
            pltpu.VMEM((2, ny, 2 * ny), BF16),
            pltpu.VMEM((2, ny, LANES), BF16),
            pltpu.VMEM((2, ny, LANES), BF16),
            pltpu.SemaphoreType.DMA((1,)),
            pltpu.SemaphoreType.DMA((parts,)),
            pltpu.SemaphoreType.DMA((1,)),
            pltpu.SemaphoreType.DMA((parts,)),
            pltpu.SemaphoreType.DMA((1,)),
            pltpu.SemaphoreType.DMA((2,)),
            pltpu.SemaphoreType.DMA((7,)),
        ],
        compiler_params=pltpu.CompilerParams(
            collective_id=0, has_side_effects=True, vmem_limit_bytes=64 * 1024 * 1024
        ),
    )(
        pixels, taps, plane_offset, grid_row, slab_of_block.reshape(1, rows // TILE),
        jnp.asarray(np.concatenate([pick_table(width, groups), rim_table(columns)])),
        jnp.asarray(transform_table(ny)),
    )


def solution(mesh, width=48, ny=512, parts=4, step=3072):
    sizes = (mesh.shape["img"], mesh.shape["gz"], mesh.shape["gy"], width, ny, parts, step)
    return jax.shard_map(
        functools.partial(local, sizes),
        mesh=mesh,
        in_specs=(
            P(None, None, ("img", "gz", "gy")),
            P(None, ("img", "gz", "gy")),
            P(("img", "gz", "gy")),
            P(("img", "gz", "gy")),
            P(("img", "gz", "gy"), None),
        ),
        out_specs=P(None, ("img", "gy"), "gz", None),
        check_vma=False,
    )
```

```python
import functools
import math

import jax
import jax.numpy as jnp
import numpy as np
from jax import lax
from jax.experimental import pallas as pl
from jax.experimental.pallas import tpu as pltpu
from jax.sharding import PartitionSpec as P

MESH = pl.DeviceIdType.MESH
F32 = jnp.float32
BF16 = jnp.bfloat16
TILE = 16
CAPACITY = 3
META = 8
LANES = 128
NT = (((1,), (1,)), ((), ()))


def transform_table(length):
    steps = np.arange(length)
    phase = (steps[:, None] * steps[None, :] % length) * (2.0 * math.pi / length)
    table = np.concatenate([np.cos(phase), np.sin(phase)], axis=1) / math.sqrt(length)
    table = table.astype(np.float32)
    high = table.astype(jnp.bfloat16)
    low = (table - high.astype(np.float32)).astype(jnp.bfloat16)
    return np.stack([high, low])


def pick_table(width, groups):
    columns = width // groups
    pick = np.zeros((groups, TILE, LANES), np.float32)
    for group in range(groups):
        for s in range(2 * columns):
            pick[group, s, (s % 2) * width + group * columns + s // 2] = 1.0
        for s in range(META):
            pick[group, 2 * columns + s, 2 * width + s] = 1.0
    return pick.reshape(groups * TILE, LANES).astype(jnp.bfloat16)


def rim_table(columns):
    place = np.zeros((LANES, LANES), np.float32)
    for x in range(columns):
        for c in range(2):
            for z in range(2):
                place[2 * columns * TILE + TILE * c + 2 * x + z, (2 * x + c) * TILE + z] = 1.0
    return place.astype(jnp.bfloat16)


def kernel(
    sizes, pix_hbm, taps_hbm, plane_hbm, row_hbm, slab_hbm, small_hbm, table_hbm, out_ref,
    pix_ref, taps_ref, plane_ref, row_ref, slab_ref, small, x_buf, send1, recv1, send2, recv2, acc, table, send3, recv3,
    s1_sem, r1_sem, s2_sem, r2_sem, s3_sem, r3_sem, in_sem,
):
    n_img, n_gz, n_gy, width, ny, parts, step = sizes
    nx_hi = 2
    nz = n_gz // nx_hi
    groups = n_img * n_gy
    columns = width // groups
    rows = pix_hbm.shape[2]
    blocks = rows // TILE
    slot_rows = CAPACITY * TILE
    part_slots = n_gz // parts
    part_rows = part_slots * slot_rows
    half = ny // 2
    reach = nz // 2
    sends = n_gz // 2
    own_send = sends - nx_hi

    img, gz, gy = lax.axis_index("img"), lax.axis_index("gz"), lax.axis_index("gy")
    my_group = img * n_gy + gy

    my_x, my_z = lax.div(gz, nz), lax.rem(gz, nz)
    my_y, my_side = lax.div(img, 2), lax.rem(img, 2)

    def slab_peer(k):
        turn, m = k % sends % nx_hi, k % sends // nx_hi
        x = lax.rem(my_x + turn, nx_hi)
        along = (reach - m) // 2 * (2 * (m % 2) - 1) + nz
        z = my_z + along + (x * reach if m == 0 else 0)
        return x * nz + lax.rem(z, nz)

    def any_peer(k):
        turn, m = k % nx_hi, nz - 1 - k // nx_hi
        along = (m + 1) // 2 * (2 * (m % 2) - 1) + nz
        return lax.rem(my_x + turn, nx_hi) * nz + lax.rem(my_z + along, nz)

    any_own = n_gz - nx_hi
    any_others = [k for k in range(n_gz) if k != any_own]

    def group_peer(e):
        core, side, along = e % n_gy, e // n_gy % 2, e // n_gy // 2
        y = lax.rem(my_y + along, n_img // 2)
        return y * 2 + lax.rem(my_side + side, 2), lax.rem(gy + core, n_gy)

    def copy1(k):
        peer = slab_peer(k)
        return pltpu.make_async_remote_copy(
            src_ref=send1.at[pl.ds(pl.multiple_of(k * slot_rows, TILE), slot_rows)],
            dst_ref=recv1.at[pl.ds(pl.multiple_of(k * slot_rows, TILE), slot_rows)],
            send_sem=s1_sem.at[0], recv_sem=r1_sem.at[k // part_slots],
            device_id=(img, peer, gy), device_id_type=MESH,
        )

    def copy2(part, e):
        to_img, to_gy = group_peer(e)
        peer = to_img * n_gy + to_gy
        return pltpu.make_async_remote_copy(
            src_ref=send2.at[part, pl.ds(pl.multiple_of(peer * TILE, TILE), TILE)],
            dst_ref=recv2.at[part, :, pl.ds(pl.multiple_of(e * part_rows, LANES), part_rows)],
            send_sem=s2_sem.at[0], recv_sem=r2_sem.at[part],
            device_id=(to_img, gz, to_gy), device_id_type=MESH,
        )

    def copy3(slab, peer):
        return pltpu.make_async_remote_copy(
            src_ref=send3.at[slab, pl.ds(pl.multiple_of(peer * TILE, TILE), TILE)],
            dst_ref=recv3.at[slab, pl.ds(pl.multiple_of(gz * TILE, TILE), TILE)],
            send_sem=s3_sem.at[0], recv_sem=r3_sem.at[slab],
            device_id=(img, peer, gy), device_id_type=MESH,
        )

    pairs = [
        (slab_hbm, slab_ref), (taps_hbm, taps_ref), (plane_hbm, plane_ref), (row_hbm, row_ref),
        (pix_hbm, pix_ref), (small_hbm, small), (table_hbm, table),
    ]
    fetches = [pltpu.make_async_copy(*pair, in_sem.at[i]) for i, pair in enumerate(pairs)]
    for fetch in fetches:
        fetch.start()

    def landed(view, sem):
        pltpu.make_async_remote_copy(
            src_ref=view, dst_ref=view, send_sem=s1_sem.at[0], recv_sem=sem,
            device_id=(img, any_peer(0), gy), device_id_type=MESH,
        ).wait_recv()

    def left(view, sem):
        pltpu.make_async_remote_copy(
            src_ref=view, dst_ref=view, send_sem=sem, recv_sem=r1_sem.at[0],
            device_id=(img, any_peer(0), gy), device_id_type=MESH,
        ).wait_send()

    def loop(first, last, do):
        def body(index, carry):
            do(index)
            return carry
        lax.fori_loop(first, last, body, 0)

    barrier = pltpu.get_barrier_semaphore()

    near = [k for k in any_others if nz - 1 - k // nx_hi <= reach]
    for k in near:
        pl.semaphore_signal(
            barrier, inc=1, device_id=(img, any_peer(k), gy), device_id_type=MESH
        )
    for e in range(1, groups):
        to_img, to_gy = group_peer(e)
        pl.semaphore_signal(barrier, inc=1, device_id=(to_img, gz, to_gy), device_id_type=MESH)

    for fetch in fetches[:5]:
        fetch.wait()
    taps = taps_ref[...].astype(F32)
    x_iota = lax.broadcasted_iota(jnp.int32, (width, rows), 0)
    for c in range(2):
        p = pix_ref[c].astype(F32)
        before = jnp.where(x_iota == 0, 0.0, pltpu.roll(p, 1, 0))
        after = jnp.where(x_iota == width - 1, 0.0, pltpu.roll(p, width - 1, 0))
        spread = taps[6:7] * before + taps[7:8] * p + taps[8:9] * after
        x_buf[c * width : (c + 1) * width] = spread.astype(BF16)
    data = jnp.concatenate(
        [
            taps[0:6], plane_ref[...].reshape(1, rows).astype(F32),
            (row_ref[...].reshape(1, rows) - half).astype(F32),
            jnp.zeros((LANES - 2 * width - META, rows), F32),
        ],
        axis=0,
    )
    x_buf[2 * width :] = data.astype(BF16)

    block_iota = lax.broadcasted_iota(jnp.int32, (blocks, rows), 0)
    row_iota = lax.broadcasted_iota(jnp.int32, (blocks, rows), 1)
    row_block = row_iota // TILE
    square = (blocks, blocks)
    diagonal = lax.broadcasted_iota(jnp.int32, square, 0) == lax.broadcasted_iota(jnp.int32, square, 1)
    target = jnp.sum(jnp.where(diagonal, slab_ref[...], 0), axis=1, keepdims=True)
    target = jnp.broadcast_to(target, (blocks, rows))
    own = jnp.sum(jnp.where(block_iota == row_block, target, 0), axis=0, keepdims=True)
    earlier = jnp.where((target == own) & (block_iota < row_block), 1, 0)
    rank = jnp.sum(earlier, axis=0, keepdims=True)
    side = own // nz
    turn = (side - gz // nz + nx_hi) % nx_hi
    along = (own % nz - gz % nz + nz + reach // 2 - side + nz) % nz
    far_owner = along // reach
    along = along % reach - reach // 2 + side
    order = jnp.where(along >= 0, jnp.maximum(reach - 1 - 2 * along, 0), reach + 2 * along)
    order = far_owner * sends + order * nx_hi + turn
    place = (order * CAPACITY + rank) * TILE + row_iota[0:1] % TILE

    slot_iota = lax.broadcasted_iota(jnp.int32, (part_rows, rows), 0)

    def part_sends(part):
        every = range(part * part_slots, (part + 1) * part_slots)
        return [k for k in every if k % sends != own_send]

    def permute(index):
        first = index * part_rows
        chosen = jnp.where(slot_iota == place - first, 1.0, 0.0).astype(BF16)
        moved = lax.dot_general(chosen, x_buf[...], NT, preferred_element_type=F32)
        send1[first : first + part_rows] = moved.astype(BF16)
        if index == 0:
            pl.semaphore_wait(barrier, len(near) + groups - 1)
        for k in part_sends(index):
            copy1(k).start()

    for part in range(parts):
        permute(part)
    for k in (own_send, own_send + sends):
        recv1[k * slot_rows : (k + 1) * slot_rows] = send1[k * slot_rows : (k + 1) * slot_rows]

    acc[...] = jnp.zeros_like(acc)
    y_iota = (lax.broadcasted_iota(jnp.int32, (half + TILE, step), 0) - half // 2).astype(BF16)
    z_iota = lax.broadcasted_iota(jnp.int32, (TILE, step), 0)
    rim_x = z_iota // 2
    rim_z = (z_iota % 2 + TILE).astype(BF16)
    z_iota = z_iota.astype(BF16)

    def spread_part(part, index):
        got = recv2[part, :, pl.ds(pl.multiple_of(index * step, step), step)]
        zero = jnp.zeros((), BF16)
        y = got[13:14].astype(F32) + (half - 1.0)
        y = jnp.where(y < 0.0, y + ny, y)
        upper = y >= half
        y = jnp.where(upper, y - half, y) - half // 2
        ys = [(y + b).astype(BF16) for b in range(3)]
        in_high = jnp.where(upper, 1.0, 0.0).astype(BF16)
        got = got.astype(BF16)
        z0 = got[12:13]
        z1, z2 = z0 + 1, z0 + 2
        along_y = jnp.where(
            y_iota == ys[0], got[9:10],
            jnp.where(y_iota == ys[1], got[10:11], jnp.where(y_iota == ys[2], got[11:12], zero)),
        ).astype(BF16)
        along_z = jnp.where(
            z_iota == z0, got[6:7],
            jnp.where(z_iota == z1, got[7:8], jnp.where(z_iota == z2, got[8:9], zero)),
        )
        rim = jnp.where(rim_z == z1, got[7:8], jnp.where(rim_z == z2, got[8:9], zero))
        values = []
        for c in range(2):
            value = jnp.zeros((TILE, step), BF16)
            for x in range(columns):
                value = jnp.where(rim_x == x, got[2 * x + c : 2 * x + c + 1], value)
            values.append(value)
        pieces = []
        for mask in (1 - in_high, in_high):
            z_part, rim_part = along_z * mask, rim * mask
            pieces += [z_part * got[s : s + 1] for s in range(2 * columns)]
            pieces += [rim_part * value for value in values]
        along_zx = jnp.concatenate([piece.astype(BF16) for piece in pieces], axis=0)
        acc[part // (parts // 2)] += lax.dot_general(along_y, along_zx, NT, preferred_element_type=F32)

    def take_part(part):
        landed(recv1.at[pl.ds(0, len(part_sends(part)) * slot_rows)], r1_sem.at[part])
        first = part * part_rows
        turned = lax.dot_general(
            small[0 : groups * TILE], recv1[first : first + part_rows], NT, preferred_element_type=F32
        )
        send2[part] = turned.astype(BF16)
        for e in reversed(range(1, groups)):
            copy2(part, e).start()
        recv2[part, :, 0:part_rows] = send2[part, pl.ds(pl.multiple_of(my_group * TILE, TILE), TILE)]

    def grid_part(part):
        landed(recv2.at[part, :, pl.ds(0, (groups - 1) * part_rows)], r2_sem.at[part])
        loop(0, groups * part_rows // step, functools.partial(spread_part, part))

    lane = lax.broadcasted_iota(jnp.int32, (ny, LANES), 1)
    here = pl.ds(pl.multiple_of(gz * TILE, TILE), TILE)

    def turn_y(slab):
        low, high = acc[slab, :half, :LANES], acc[slab, :half, LANES:]
        low_rim, high_rim = acc[slab, half:, :LANES], acc[slab, half:, LANES:]
        grid = jnp.concatenate(
            [low[:TILE] + high_rim, low[TILE:], high[:TILE] + low_rim, high[TILE:]], axis=0
        )
        other = jnp.where(
            (lane // TILE) % 2 == 0, -pltpu.roll(grid, LANES - TILE, 1), pltpu.roll(grid, TILE, 1)
        )
        both = jnp.concatenate([grid, other], axis=0)
        both_high = both.astype(BF16)
        both_low = (both - both_high.astype(F32)).astype(BF16)
        both_bits = jnp.concatenate([both_high, both_low], axis=1)
        wide = jnp.dot(table[0], both_bits, preferred_element_type=F32)
        turned = wide[:, :LANES] + wide[:, LANES:]
        turned = turned + jnp.dot(table[1], both_high, preferred_element_type=F32)
        send3[slab] = turned.astype(BF16)
        @pl.when(slab == 0)
        def _():
            for k in any_others:
                copy3(0, any_peer(k)).start()

        @pl.when(slab == 1)
        def _():
            for z in range(nz):
                for x in range(nx_hi):
                    peer = x * nz + z

                    @pl.when(gz != peer)
                    def _():
                        copy3(1, peer).start()

        recv3[slab, here] = send3[slab, here]

    fetches[5].wait()
    fetches[6].wait()
    per_slab = parts // 2
    for part in range(parts):
        take_part(part)

    def slab_step(slab):
        grid_part(slab * per_slab)

        loop(slab * per_slab + 1, (slab + 1) * per_slab, grid_part)
        turn_y(slab)

    loop(0, 2, slab_step)
    left(send1.at[pl.ds(0, (n_gz - 2) * slot_rows)], s1_sem.at[0])
    left(recv2.at[:, :, pl.ds(0, (groups - 1) * part_rows)], s2_sem.at[0])

    landed(recv3.at[0, pl.ds(0, (n_gz - 1) * TILE)], r3_sem.at[0])
    got = recv3[0]
    place_rim = small[groups * TILE :]
    past = jnp.dot(got, place_rim, preferred_element_type=F32)
    landed(recv3.at[1, pl.ds(0, (n_gz - 1) * TILE)], r3_sem.at[1])
    span = reach * TILE
    swapped = [recv3[1, (2 * x + 1 - i) * span : (2 * x + 2 - i) * span] for x in range(nx_hi) for i in range(2)]
    swapped = jnp.concatenate(swapped, axis=0)
    past = past + jnp.dot(swapped, place_rim, preferred_element_type=F32)
    planes = got.astype(F32) + swapped.astype(F32) + jnp.concatenate([past[-TILE:], past[:-TILE]], axis=0)
    per = LANES // TILE
    spot = lax.broadcasted_iota(jnp.int32, (TILE, LANES), 1) // TILE
    ordered = []
    for s in range(2 * columns):
        across = []
        for t in range(n_gz // per):
            value = jnp.zeros((TILE, LANES), F32)
            for j in range(per):
                first = (t * per + j) * TILE
                tile = planes[first : first + TILE]
                turn = (j - s) * TILE % LANES
                tile = pltpu.roll(tile, turn, 1) if turn else tile
                value = jnp.where(spot == j, tile, value)
            across.append(value)
        ordered.append(jnp.concatenate(across, axis=1))
    ordered = jnp.concatenate(ordered, axis=0)
    ordered_high = ordered.astype(BF16)
    ordered_low = (ordered - ordered_high.astype(F32)).astype(BF16)
    ordered_bits = jnp.concatenate([ordered_high, ordered_low], axis=0)
    lines = ordered.shape[0]
    wide = jnp.dot(ordered_bits, table[0], preferred_element_type=F32)
    volume = wide[:lines] + wide[lines:]
    volume = volume + jnp.dot(ordered_high, table[1], preferred_element_type=F32)
    for x in range(columns):
        real = volume[2 * x * TILE : (2 * x + 1) * TILE]
        imag = volume[(2 * x + 1) * TILE : (2 * x + 2) * TILE]
        out_ref[0, x] = real[:, :ny] - imag[:, ny:]
        out_ref[1, x] = real[:, ny:] + imag[:, :ny]
    left(recv3.at[:, pl.ds(0, (n_gz - 1) * TILE)], s3_sem.at[0])


def local(sizes, pixels, taps, plane_offset, grid_row, slab_of_block):
    n_img, n_gz, n_gy, width, ny, parts, step = sizes
    groups = n_img * n_gy
    columns = width // groups
    rows = pixels.shape[2]
    slots = n_gz * CAPACITY * TILE
    vmem = pl.BlockSpec(memory_space=pltpu.VMEM)
    return pl.pallas_call(
        functools.partial(kernel, sizes),
        out_shape=jax.ShapeDtypeStruct((2, columns, ny // n_gz, ny), F32),
        in_specs=[pl.BlockSpec(memory_space=pl.ANY)] * 7,
        out_specs=vmem,
        scratch_shapes=[
            pltpu.VMEM((2, width, rows), BF16),
            pltpu.VMEM((taps.shape[0], rows), BF16),
            pltpu.VMEM((rows,), jnp.int32),
            pltpu.VMEM((rows,), jnp.int32),
            pltpu.VMEM((1, rows // TILE), jnp.int32),
            pltpu.VMEM((groups * TILE + LANES, LANES), BF16),
            pltpu.VMEM((LANES, rows), BF16),
            pltpu.VMEM((slots, LANES), BF16),
            pltpu.VMEM((slots, LANES), BF16),
            pltpu.VMEM((parts, groups * TILE, slots // parts), BF16),
            pltpu.VMEM((parts, TILE, groups * slots // parts), BF16),
            pltpu.VMEM((2, ny // 2 + TILE, 2 * LANES), F32),
            pltpu.VMEM((2, ny, 2 * ny), BF16),
            pltpu.VMEM((2, ny, LANES), BF16),
            pltpu.VMEM((2, ny, LANES), BF16),
            pltpu.SemaphoreType.DMA((1,)),
            pltpu.SemaphoreType.DMA((parts,)),
            pltpu.SemaphoreType.DMA((1,)),
            pltpu.SemaphoreType.DMA((parts,)),
            pltpu.SemaphoreType.DMA((1,)),
            pltpu.SemaphoreType.DMA((2,)),
            pltpu.SemaphoreType.DMA((7,)),
        ],
        compiler_params=pltpu.CompilerParams(
            collective_id=0, has_side_effects=True, vmem_limit_bytes=64 * 1024 * 1024
        ),
    )(
        pixels, taps, plane_offset, grid_row, slab_of_block.reshape(1, rows // TILE),
        jnp.asarray(np.concatenate([pick_table(width, groups), rim_table(columns)])),
        jnp.asarray(transform_table(ny)),
    )


def solution(mesh, width=48, ny=512, parts=4, step=3072):
    sizes = (mesh.shape["img"], mesh.shape["gz"], mesh.shape["gy"], width, ny, parts, step)
    return jax.shard_map(
        functools.partial(local, sizes),
        mesh=mesh,
        in_specs=(
            P(None, None, ("img", "gz", "gy")),
            P(None, ("img", "gz", "gy")),
            P(("img", "gz", "gy")),
            P(("img", "gz", "gy")),
            P(("img", "gz", "gy"), None),
        ),
        out_specs=P(None, ("img", "gy"), "gz", None),
        check_vma=False,
    )
```
